32 devices in a mesh: rep: 2 (over core), fsdp: 16 (over z, y, x).
Axes of the slice: x: 2, y: 2, z: 4, core: 2. Of those that a mesh axis runs over, the one named last changes fastest.
Arguments:
- tokens: bfloat16 [16384, 768], P(('rep', 'fsdp')), may hold values from -6 to 6
- modality: int32 [16384, 3], P(('rep', 'fsdp')), may hold values from 0 to 1, as said below
- lengths: int32 [64], P(('rep', 'fsdp')), may hold values from 64 to 256, as said below
- ln1_gain: bfloat16 [768], P('fsdp'), may hold values from 0.5 to 1.5
- ln1_bias: bfloat16 [768], P('fsdp'), may hold values from -3 to 3
- w_qkv: bfloat16 [768, 2304], P('fsdp'), may hold values from -0.21875 to 0.21875
- w_out: bfloat16 [768, 768], P('fsdp'), may hold values from -0.875 to 0.875
- out_bias: bfloat16 [768], P('fsdp'), may hold values from -3 to 3
- ln2_gain: bfloat16 [768], P('fsdp'), may hold values from 0.5 to 1.5
- ln2_bias: bfloat16 [768], P('fsdp'), may hold values from -3 to 3
- w_in: bfloat16 [3, 768, 3072], P(None, 'fsdp'), may hold values from -0.21875 to 0.21875
- in_bias: bfloat16 [3, 3072], P(None, 'fsdp'), may hold values from -3 to 3
- w_back: bfloat16 [3, 3072, 768], P(None, 'fsdp'), may hold values from -0.109375 to 0.109375
- back_bias: bfloat16 [3, 768], P(None, 'fsdp'), may hold values from -3 to 3
- cotangent: bfloat16 [16384, 768], P(('rep', 'fsdp')), may hold values from -6 to 6
Outputs:
- output: bfloat16 [16384, 768], P(('rep', 'fsdp'))
- grad_tokens: bfloat16 [16384, 768], P(('rep', 'fsdp'))
- grad_ln1_gain: float32 [768], P('fsdp')
- grad_ln1_bias: float32 [768], P('fsdp')
- grad_w_qkv: float32 [768, 2304], P('fsdp')
- grad_w_out: float32 [768, 768], P('fsdp')
- grad_out_bias: float32 [768], P('fsdp')
- grad_ln2_gain: float32 [768], P('fsdp')
- grad_ln2_bias: float32 [768], P('fsdp')
- grad_w_in: float32 [3, 768, 3072], P(None, 'fsdp')
- grad_in_bias: float32 [3, 3072], P(None, 'fsdp')
- grad_w_back: float32 [3, 3072, 768], P(None, 'fsdp')
- grad_back_bias: float32 [3, 768], P(None, 'fsdp')
The draws below stay inside these ranges and needn't reach their ends.
Inputs may be any that keep to these rules, and one draw needn't show every extreme that they name: `modality`: each row has exactly one 1; columns are vision, language and joining. `lengths`: the largest is 256 in every draw.
All inputs are finite; a program needn't handle non-finite values.
Results may differ from the reference program's by a relative error of at most 0.02.
Values may be sent and summed in bfloat16 or wider, within the bound.
No kernel may reach another device: no remote copies, remote signals or barrier semaphores. Data moves between devices by JAX's collectives and lax.ppermute only.
A program may use at most 256 MiB of HBM per device.

```python
import math
import jax
import jax.numpy as jnp
from jax import lax

D = 768
HEADS = 12
HEAD_DIM = 64
FF = 3072
EXPERTS = 3
SEQ = 256
SEQS = 64
TOKENS = 16384


def draw_modality(key, part):
    chosen = jax.random.randint(key, (TOKENS,), 0, EXPERTS)
    return (chosen[:, None] == jnp.arange(EXPERTS, dtype=jnp.int32)[None, :]).astype(jnp.int32)


def draw_lengths(key, part):
    drawn_len = jax.random.randint(key, (SEQS,), SEQ // 4, SEQ + 1)
    return drawn_len.at[0].set(SEQ).astype(jnp.int32)


def steps_of(rng, extent, cuts, low, high):
    loudness, own = 1.0, jax.random.fold_in(rng, 6)
    for dim, blocks in cuts:
        draws = jnp.exp(jax.random.uniform(jax.random.fold_in(own, dim), (blocks,), jnp.float32, low / len(cuts), high / len(cuts)))
        loudness = loudness * jnp.repeat(draws, extent[dim] // blocks).reshape([-1 if axis == dim else 1 for axis in range(len(extent))])
    return loudness


def scatter_about(stream_key, shape, deviation, most, pieces=(), kind=jnp.bfloat16):
    gain = steps_of(stream_key, shape, pieces, -0.22, 0.18) if pieces else 1.0
    drawn = jax.random.normal(stream_key, shape, jnp.float32) * deviation * gain
    return jnp.minimum(jnp.maximum(drawn, -most), most).astype(kind)


def setup_inputs(seed: int = 0) -> dict:
    splits = jax.random.split(jax.random.key(seed), 16)
    return {
        "tokens": scatter_about(splits[0], (TOKENS, D), 1.0, 6.0, ((0, 32),)),
        "modality": draw_modality(jax.random.fold_in(splits[15], 71), 0),
        "lengths": draw_lengths(jax.random.fold_in(splits[15], 71), 0),
        "ln1_gain": jnp.clip(1.0 + 0.1 * jax.random.normal(splits[3], (D,), jnp.float32), 0.5, 1.5).astype(jnp.bfloat16),
        "ln1_bias": scatter_about(splits[4], (D,), 0.5, 3.0, ((0, 16),)),
        "w_qkv": scatter_about(splits[5], (D, 3 * D), D ** -0.5, 0.21875, ((0, 16),)),
        "w_out": scatter_about(splits[6], (D, D), (D // 16) ** -0.5, 0.875, ((0, 16),)),
        "out_bias": scatter_about(splits[7], (D,), 0.5, 3.0, ((0, 16),)),
        "ln2_gain": jnp.clip(1.0 + 0.1 * jax.random.normal(splits[8], (D,), jnp.float32), 0.5, 1.5).astype(jnp.bfloat16),
        "ln2_bias": scatter_about(splits[9], (D,), 0.5, 3.0, ((0, 16),)),
        "w_in": scatter_about(splits[10], (EXPERTS, D, FF), D ** -0.5, 0.21875, ((1, 16),)),
        "in_bias": scatter_about(splits[11], (EXPERTS, FF), 0.5, 3.0, ((1, 16),)),
        "w_back": scatter_about(splits[12], (EXPERTS, FF, D), FF ** -0.5, 0.109375, ((1, 16),)),
        "back_bias": scatter_about(splits[13], (EXPERTS, D), 0.5, 3.0, ((1, 16),)),
        "cotangent": scatter_about(splits[14], (TOKENS, D), 1.0, 6.0, ((0, 32),)),
    }


@jax.custom_vjp
def low(v):
    return lax.optimization_barrier(v.astype(jnp.bfloat16)).astype(jnp.float32)

@jax.custom_vjp
def low_back(v):
    return v

def low_keep(v):
    return (low(v), None)

def low_pass(kept, grad):
    return (grad,)

def back_keep(v):
    return (v, None)

def back_low(kept, grad):
    return (low(grad),)
low.defvjp(low_keep, low_pass)
low_back.defvjp(back_keep, back_low)

def layer_norm(values, norm_gain, norm_bias):
    average = lax.optimization_barrier(jnp.mean(values, axis=-1, keepdims=True))
    centred = values - average
    spread = lax.optimization_barrier(jnp.mean(centred * centred, axis=-1, keepdims=True))
    return centred * lax.rsqrt(spread + 1e-05) * norm_gain + norm_bias

def block_forward(params, inputs_blk, modality_blk, lengths_blk):
    ln1_gain, ln1_bias, w_qkv, w_out, out_bias, ln2_gain, ln2_bias, w_in, in_bias, w_back, back_bias = params
    highest = lax.Precision.HIGHEST
    row_count = inputs_blk.shape[0]
    seq_count = row_count // SEQ
    normed_one = low(layer_norm(inputs_blk, ln1_gain, ln1_bias))
    packed = low_back(low(jnp.dot(normed_one, w_qkv, precision=highest)))
    packed = packed.reshape(seq_count, SEQ, 3, HEADS, HEAD_DIM)
    query_part = packed[:, :, 0]
    key_part = packed[:, :, 1]
    value_part = packed[:, :, 2]
    scores = jnp.einsum('sqhd,skhd->shqk', query_part, key_part, precision=highest) * HEAD_DIM ** (-0.5)
    positions = jnp.arange(SEQ, dtype=jnp.int32)
    valid = positions[None, :] < lengths_blk[:, None]
    scores = jnp.where(valid[:, None, None, :], scores, -1e+30)
    scores = low_back(scores)
    probs = low(jax.nn.softmax(scores, axis=-1))
    mixed = jnp.einsum('shqk,skhd->sqhd', probs, value_part, precision=highest).reshape(row_count, D)
    mixed = low_back(low(mixed))
    branch = low_back(jnp.dot(mixed, w_out, precision=highest) + out_bias)
    middle = inputs_blk + branch
    normed_two = low(layer_norm(middle, ln2_gain, ln2_bias))
    pre = low_back(jnp.einsum('td,edf->etf', normed_two, w_in, precision=highest) + in_bias[:, None, :])
    act = low(jax.nn.gelu(pre, approximate=False))
    expert_out = jnp.einsum('etf,efd->etd', act, w_back, precision=highest) + back_bias[:, None, :]
    return middle + jnp.einsum('te,etd->td', modality_blk, expert_out, precision=highest)

def reference(tokens, modality, lengths, ln1_gain, ln1_bias, w_qkv, w_out, out_bias, ln2_gain, ln2_bias, w_in, in_bias, w_back, back_bias, cotangent):
    params = tuple((item.astype(jnp.float32) for item in (ln1_gain, ln1_bias, w_qkv, w_out, out_bias, ln2_gain, ln2_bias, w_in, in_bias, w_back, back_bias)))
    group = math.gcd(SEQS, max(1, 4096 // SEQ))
    row_block = group * SEQ
    block_count = SEQS // group
    inputs_all = tokens.astype(jnp.float32).reshape(block_count, row_block, D)
    modality_all = modality.astype(jnp.float32).reshape(block_count, row_block, EXPERTS)
    lengths_all = lengths.astype(jnp.int32).reshape(block_count, group)
    cot_all = cotangent.astype(jnp.float32).reshape(block_count, row_block, D)

    def step_block(totals, item):
        inputs_blk, modality_blk, lengths_blk, cot_blk = item

        def forward_only(weights, inputs_here):
            return block_forward(weights, inputs_here, modality_blk, lengths_blk)
        result, pull = jax.vjp(forward_only, params, inputs_blk)
        grad_params, grad_inputs = pull(cot_blk)
        totals = jax.tree.map(lambda left, right: left + right, totals, grad_params)
        return (totals, (result.astype(jnp.bfloat16), grad_inputs.astype(jnp.bfloat16)))
    zeros = jax.tree.map(jnp.zeros_like, params)
    totals, (results, grads) = lax.scan(step_block, zeros, (inputs_all, modality_all, lengths_all, cot_all))
    return (results.reshape(TOKENS, D), grads.reshape(TOKENS, D), totals[0], totals[1], totals[2], totals[3], totals[4], totals[5], totals[6], totals[7], totals[8], totals[9], totals[10])
```

```python
import functools
import math

import jax
import jax.numpy as jnp
from jax import lax
from jax.experimental import pallas as pl
from jax.experimental.pallas import tpu as pltpu
from jax.sharding import Mesh
from jax.sharding import PartitionSpec as P

HEADS = 12
HEAD_DIM = 64
SEQ = 256
D = 768
EXPERTS = 3
UNIT = 16
TILE = 256
UNITS = TILE // UNIT

INV_ROOT_TWO = 1.0 / math.sqrt(2.0)
INV_ROOT_TAU = 1.0 / math.sqrt(2.0 * math.pi)
F32 = jnp.float32
BF16 = jnp.bfloat16

VMEM = pl.BlockSpec(memory_space=pltpu.VMEM)
SMEM = pl.BlockSpec(memory_space=pltpu.SMEM)
ANY = pl.BlockSpec(memory_space=pl.ANY)


def dot(a, b):
    return lax.dot_general(a, b, (((1,), (0,)), ((), ())), preferred_element_type=F32)


def dot_nt(a, b):
    return lax.dot_general(a, b, (((1,), (1,)), ((), ())), preferred_element_type=F32)


def dot_tn(a, b):
    return lax.dot_general(a, b, (((0,), (0,)), ((), ())), preferred_element_type=F32)


def norm_stats(values):
    average = jnp.mean(values, axis=-1, keepdims=True)
    centred = values - average
    inverse = lax.rsqrt(jnp.mean(centred * centred, axis=-1, keepdims=True) + 1e-05)
    return centred * inverse, inverse


def norm_backward(weighted, scaled, inverse):
    first = jnp.mean(weighted, axis=-1, keepdims=True)
    second = jnp.mean(weighted * scaled, axis=-1, keepdims=True)
    return inverse * (weighted - first - scaled * second)


def two_heads(block):
    low = lax.broadcasted_iota(jnp.int32, block.shape, 1) < HEAD_DIM
    nothing = jnp.zeros_like(block)
    return jnp.concatenate([jnp.where(low, block, nothing), jnp.where(low, nothing, block)], axis=0)


def merge_heads(block):
    low = lax.broadcasted_iota(jnp.int32, (SEQ, 2 * HEAD_DIM), 1) < HEAD_DIM
    return jnp.where(low, block[:SEQ], block[SEQ:])


PAIRS = HEADS // 2


def attn_fwd_kernel(share, where_ref, len_ref, tok_ref, vec_ref, perm_ref, *rest):
    pieces = rest[:8]
    mid_ref, xs_ref, q_ref, k_ref, v_ref, mixed_ref, probs_ref, w_ref = rest[8:16]
    sems = rest[16]
    core, y, x = where_ref[0], where_ref[1], where_ref[2]
    depth = pieces[0].shape[0]
    copies = []
    for matrix in range(2):
        for n, piece in enumerate(pieces):
            far, y_of, x_of = n // 4, (n // 2) % 2, n % 2
            slot = 2 * jnp.where(far == 1, 1 - core, core) + matrix
            place = 2 * jnp.where(y_of == 1, 1 - y, y) + jnp.where(x_of == 1, 1 - x, x)
            for z in range(depth):
                row = pl.multiple_of((4 * z + place) * share, share)
                first = matrix * (share + 8)
                copies.append(pltpu.make_async_copy(
                    piece.at[z, pl.ds(first, share)], w_ref.at[slot, pl.ds(row, share)],
                    sems.at[matrix, n, z]))
    for copy in copies:
        copy.start()
    values = tok_ref[...].astype(F32)
    scaled, _ = norm_stats(values)
    normed = (scaled * vec_ref[0:1, :] + vec_ref[1:2, :]).astype(BF16)
    for copy in copies:
        copy.wait()
    q_ref[...] = dot(normed, w_ref[0]).astype(BF16)
    k_ref[...] = dot(normed, w_ref[1]).astype(BF16)
    v_ref[...] = dot(normed, w_ref[2]).astype(BF16)
    seqs = tok_ref.shape[0] // SEQ
    for seq in range(seqs):
        length = len_ref[seq]
        rows = slice(seq * SEQ, (seq + 1) * SEQ)

        def step(pair, carry):
            cols = pl.ds(pl.multiple_of(pair * 128, 128), 128)
            both = two_heads(q_ref[rows, cols])
            scores = dot_nt(both, k_ref[rows, cols]) * (HEAD_DIM ** -0.5)
            valid = lax.broadcasted_iota(jnp.int32, scores.shape, 1) < length
            scores = jnp.where(valid, scores, -1e30)
            top = jnp.max(scores, axis=-1, keepdims=True)
            grown = jnp.exp(scores - top)
            total = jnp.sum(grown, axis=-1, keepdims=True)
            probs = (grown * (1.0 / total)).astype(BF16)
            probs_ref[seq * PAIRS + pair] = probs
            mixed_ref[rows, cols] = merge_heads(dot(probs, v_ref[rows, cols])).astype(BF16)
            return carry

        lax.fori_loop(0, PAIRS, step, 0)
    middle = values + dot(mixed_ref[...], w_ref[3]) + vec_ref[2:3, :]
    mid_ref[...] = middle
    scaled_two, _ = norm_stats(middle)
    normed_two = (scaled_two * vec_ref[3:4, :] + vec_ref[4:5, :]).astype(BF16)
    xs_ref[...] = dot(perm_ref[...], normed_two).astype(BF16)


def attn_fwd(where, lengths, tokens, vec, perm, pieces, share):
    rows = tokens.shape[0]
    seqs = rows // SEQ
    low = jax.ShapeDtypeStruct((rows, D), BF16)
    return pl.pallas_call(
        functools.partial(attn_fwd_kernel, share),
        out_shape=(
            jax.ShapeDtypeStruct((rows, D), F32),
            jax.ShapeDtypeStruct((perm.shape[0], D), BF16),
            low, low, low, low,
            jax.ShapeDtypeStruct((seqs * PAIRS, 2 * SEQ, SEQ), BF16),
            jax.ShapeDtypeStruct((4, D, D), BF16),
        ),
        in_specs=[SMEM] * 2 + [VMEM] * 3 + [ANY] * 8,
        out_specs=(VMEM,) * 8,
        scratch_shapes=[pltpu.SemaphoreType.DMA((2, 8, pieces[0].shape[0]))],
        compiler_params=pltpu.CompilerParams(vmem_limit_bytes=48 * 1024 * 1024),
        cost_estimate=pl.CostEstimate(flops=2 * rows * D * D * 5, bytes_accessed=14 * 1024 * 1024, transcendentals=0),
        name="attn_fwd",
    )(where, lengths, tokens, vec, perm, *pieces)


def ffn_kernel(first, tab_ref, tot_ref, where_ref, *rest):
    xs, cs, ws, b_ref = rest[0:4], rest[4:8], rest[8:10], rest[10]
    rest = rest[11:] if first else rest[15:]
    outs, (mine_ref, other_ref, gb_ref) = rest[:4], rest[4:7]
    xv, cv, wi, wb, gwi, gwb, xt, ct, ot, dt, in_sems, w_sems, out_sems = rest[7:]
    y = where_ref[1]
    depth, height = ws[0].shape[0], ws[0].shape[1] // 2
    size = xs[0].shape[0]
    weights, tokens = [], []
    for n, piece in enumerate(ws):
        y_of = y if n == 0 else 1 - y
        for z in range(depth):
            row = pl.multiple_of((2 * z + y_of) * height, height)
            for part, target in enumerate((wi, wb)):
                weights.append(pltpu.make_async_copy(
                    piece.at[z, pl.ds(part * height, height)], target.at[pl.ds(row, height)],
                    w_sems.at[n, z, part]))
    for n in range(4):
        tokens.append(pltpu.make_async_copy(xs[n], xv.at[pl.ds(n * size, size)], in_sems.at[0, n]))
        tokens.append(pltpu.make_async_copy(cs[n], cv.at[pl.ds(n * size, size)], in_sems.at[1, n]))
    for copy in tokens + weights:
        copy.start()
    gwi[...] = jnp.zeros_like(gwi)
    gwb[...] = jnp.zeros_like(gwb)
    gb_ref[...] = jnp.zeros_like(gb_ref)
    for copy in tokens + weights:
        copy.wait()
    total = tot_ref[0]
    border = 2 * size // UNIT

    def move(t, u, act):
        unit = t * UNITS + u
        held = slice(u * UNIT, (u + 1) * UNIT)
        for n, source in enumerate((ot, dt)):
            @pl.when(unit < total)
            def _():
                dst = tab_ref[unit]

                @pl.when(dst < border)
                def _():
                    act(pltpu.make_async_copy(
                        source.at[held], outs[2 * n].at[pl.ds(pl.multiple_of(dst * UNIT, UNIT), UNIT)],
                        out_sems.at[n, u]))

                @pl.when(dst >= border)
                def _():
                    act(pltpu.make_async_copy(
                        source.at[held], outs[2 * n + 1].at[pl.ds(pl.multiple_of((dst - border) * UNIT, UNIT), UNIT)],
                        out_sems.at[n, u]))

    def tile(t, carry):
        for u in range(UNITS):
            src = pl.multiple_of(tab_ref[t * UNITS + u] * UNIT, UNIT)
            xt[u * UNIT:(u + 1) * UNIT, :] = xv[pl.ds(src, UNIT), :]
            ct[u * UNIT:(u + 1) * UNIT, :] = cv[pl.ds(src, UNIT), :]
        left = (total - t * UNITS) * UNIT
        row = lax.broadcasted_iota(jnp.int32, (TILE, D), 0)
        part = jnp.where(row < left, ct[...], jnp.zeros_like(ct))
        pre = dot(xt[...], wi[...]) + b_ref[...]
        share = 0.5 * (1.0 + lax.erf(pre * INV_ROOT_TWO))
        act = (pre * share).astype(BF16)
        slope = share + pre * jnp.exp(-0.5 * pre * pre) * INV_ROOT_TAU

        @pl.when(t > 0)
        def _():
            for u in range(UNITS):
                move(t - 1, u, lambda copy: copy.wait())

        ot[...] = dot(act, wb[...]).astype(BF16)
        pre_grad = (dot_nt(part, wb[...]) * slope).astype(BF16)
        dt[...] = dot_nt(pre_grad, wi[...]).astype(BF16)
        for u in range(UNITS):
            move(t, u, lambda copy: copy.start())
        gwb[...] += dot_tn(act, part)
        gwi[...] += dot_tn(xt[...], pre_grad)
        gb_ref[...] += jnp.sum(pre_grad.astype(F32), axis=0, keepdims=True)
        return carry

    tiles = (total + UNITS - 1) // UNITS
    lax.fori_loop(0, tiles, tile, 0)

    @pl.when(tiles > 0)
    def _():
        for u in range(UNITS):
            move(tiles - 1, u, lambda copy: copy.wait())

    for z in range(depth):
        for y_of in range(2):
            rows = slice((2 * z + y_of) * height, (2 * z + y_of + 1) * height)
            for flag, target in ((y == y_of, mine_ref), (y != y_of, other_ref)):
                @pl.when(flag)
                def _():
                    target[z, :height, :] = gwi[rows, :].astype(BF16)
                    target[z, height:, :] = gwb[rows, :].astype(BF16)


def ffn(table, total, where, xs, cs, weights, bias, before):
    size = xs[0].shape[0]
    first = before is None
    quarter = bias.shape[1]
    tokens = jax.ShapeDtypeStruct((2 * size, D), BF16)
    grads = jax.ShapeDtypeStruct(weights[0].shape, BF16)
    args = [table, total, where, *xs, *cs, *weights, bias] + ([] if first else list(before))
    return pl.pallas_call(
        functools.partial(ffn_kernel, first),
        out_shape=(tokens,) * 4 + (grads, grads, jax.ShapeDtypeStruct((1, quarter), F32)),
        in_specs=[SMEM] * 3 + [ANY] * 10 + [VMEM] + [ANY] * (0 if first else 4),
        out_specs=(ANY,) * 4 + (VMEM,) * 3,
        scratch_shapes=[
            pltpu.VMEM((4 * size, D), BF16),
            pltpu.VMEM((4 * size, D), BF16),
            pltpu.VMEM((D, quarter), BF16),
            pltpu.VMEM((quarter, D), BF16),
            pltpu.VMEM((D, quarter), F32),
            pltpu.VMEM((quarter, D), F32),
            pltpu.VMEM((TILE, D), BF16),
            pltpu.VMEM((TILE, D), BF16),
            pltpu.VMEM((TILE, D), BF16),
            pltpu.VMEM((TILE, D), BF16),
            pltpu.SemaphoreType.DMA((2, 4)),
            pltpu.SemaphoreType.DMA((2, weights[0].shape[0], 2)),
            pltpu.SemaphoreType.DMA((2, UNITS)),
        ],
        input_output_aliases={} if first else {14 + i: i for i in range(4)},
        compiler_params=pltpu.CompilerParams(vmem_limit_bytes=48 * 1024 * 1024),
        cost_estimate=pl.CostEstimate(flops=12 * 1024 * D * quarter, bytes_accessed=20 * 1024 * 1024, transcendentals=0),
        name="ffn",
    )(*args)


def attn_bwd_kernel(core_ref, tok_ref, cot_ref, mid_ref, dxs_ref, unperm_ref, q_ref, k_ref, v_ref, mixed_ref,
                    probs_ref, vec_ref, hot_ref, w_ref,
                    gtok_ref, keep_ref, send_ref, gvec_ref,
                    mg, mxg, dq, dk, dv):
    norm2_grad = dot(unperm_ref[...], dxs_ref[...])
    scaled_two, inverse_two = norm_stats(mid_ref[...])
    gvec_ref[3:4, :] = jnp.sum(norm2_grad * scaled_two, axis=0, keepdims=True)
    gvec_ref[4:5, :] = jnp.sum(norm2_grad, axis=0, keepdims=True)
    mid_grad = cot_ref[...].astype(F32) + norm_backward(norm2_grad * vec_ref[3:4, :], scaled_two, inverse_two)
    mg[...] = mid_grad
    branch = mid_grad.astype(BF16)
    gvec_ref[2:3, :] = jnp.sum(branch.astype(F32), axis=0, keepdims=True)
    gvec_ref[5:8, :] = dot(hot_ref[...], cot_ref[...])[:3]
    core = core_ref[0]

    def put(matrix, value):
        low = value.astype(BF16)

        @pl.when(core == matrix // 2)
        def _():
            keep_ref[matrix % 2] = low

        @pl.when(core != matrix // 2)
        def _():
            send_ref[matrix % 2] = low

    put(3, dot_tn(mixed_ref[...], branch))
    mxg[...] = dot_nt(branch, w_ref[3]).astype(BF16)
    seqs = tok_ref.shape[0] // SEQ
    scale = HEAD_DIM ** -0.5
    for seq in range(seqs):
        rows = slice(seq * SEQ, (seq + 1) * SEQ)

        def step(pair, carry):
            cols = pl.ds(pl.multiple_of(pair * 128, 128), 128)
            probs = probs_ref[seq * PAIRS + pair]
            grads = two_heads(mxg[rows, cols])
            dv[rows, cols] = dot_tn(probs, grads).astype(BF16)
            prob_grad = dot_nt(grads, v_ref[rows, cols])
            wide = probs.astype(F32)
            inner = jnp.sum(wide * prob_grad, axis=-1, keepdims=True)
            score_grad = (wide * (prob_grad - inner)).astype(BF16)
            dq[rows, cols] = (merge_heads(dot(score_grad, k_ref[rows, cols])) * scale).astype(BF16)
            dk[rows, cols] = (dot_tn(score_grad, two_heads(q_ref[rows, cols])) * scale).astype(BF16)
            return carry

        lax.fori_loop(0, PAIRS, step, 0)
    scaled, inverse = norm_stats(tok_ref[...].astype(F32))
    normed = (scaled * vec_ref[0:1, :] + vec_ref[1:2, :]).astype(BF16)
    put(0, dot_tn(normed, dq[...]))
    put(1, dot_tn(normed, dk[...]))
    put(2, dot_tn(normed, dv[...]))
    norm1_grad = dot_nt(dq[...], w_ref[0]) + dot_nt(dk[...], w_ref[1]) + dot_nt(dv[...], w_ref[2])
    gvec_ref[0:1, :] = jnp.sum(norm1_grad * scaled, axis=0, keepdims=True)
    gvec_ref[1:2, :] = jnp.sum(norm1_grad, axis=0, keepdims=True)
    gtok_ref[...] = (mg[...] + norm_backward(norm1_grad * vec_ref[0:1, :], scaled, inverse)).astype(BF16)


def attn_bwd(core, tokens, cot, middle, dxs, unperm, q, k, v, mixed, probs, vec, hot, weights):
    rows = tokens.shape[0]
    return pl.pallas_call(
        attn_bwd_kernel,
        out_shape=(
            jax.ShapeDtypeStruct((rows, D), BF16),
            jax.ShapeDtypeStruct((2, D, D), BF16),
            jax.ShapeDtypeStruct((2, D, D), BF16),
            jax.ShapeDtypeStruct((8, D), F32),
        ),
        in_specs=[SMEM] + [VMEM] * 13,
        out_specs=(VMEM,) * 4,
        scratch_shapes=[pltpu.VMEM((rows, D), F32)] + [pltpu.VMEM((rows, D), BF16)] * 4,
        compiler_params=pltpu.CompilerParams(vmem_limit_bytes=48 * 1024 * 1024),
        cost_estimate=pl.CostEstimate(flops=2 * rows * D * D * 10, bytes_accessed=20 * 1024 * 1024, transcendentals=0),
        name="attn_bwd",
    )(core, tokens, cot, middle, dxs, unperm, q, k, v, mixed, probs, vec, hot, weights)


def swap(value, axis):
    return lax.ppermute(value, axis, [(0, 1), (1, 0)])


def diagonal(value):
    return lax.ppermute(value, ("y", "x"), [(i, 3 - i) for i in range(4)])


def after_kernel(value_ref, other_ref, out_ref):
    pass


def after(value, other):
    return pl.pallas_call(
        after_kernel,
        out_shape=jax.ShapeDtypeStruct(value.shape, value.dtype),
        in_specs=[ANY, ANY],
        out_specs=ANY,
        input_output_aliases={0: 0},
        name="after",
    )(value, other)


def ordered(mine, other, index, axis):
    first = jnp.where(index == 0, mine, other)
    second = jnp.where(index == 0, other, mine)
    return jnp.stack([first, second], axis=axis)


def spread(block, count):
    return lax.all_to_all(jnp.broadcast_to(block[None], (count,) + block.shape), "z", 0, 0, tiled=True)


def halves(value, index, axis):
    mine = lax.dynamic_index_in_dim(value, index, axis, keepdims=False)
    other = lax.dynamic_index_in_dim(value, 1 - index, axis, keepdims=False)
    return mine, other


def running(values, axis):
    steps = [lax.index_in_dim(values, 0, axis, keepdims=False)]
    for i in range(1, values.shape[axis]):
        steps.append(steps[-1] + lax.index_in_dim(values, i, axis, keepdims=False))
    return jnp.stack(steps, axis=axis)


def add_low(a, b):
    return (a.astype(F32) + b.astype(F32)).astype(BF16)


def body(outer, depth, tokens, modality, lengths, ln1_gain, ln1_bias, w_qkv, w_out, out_bias, ln2_gain, ln2_bias,
         w_in, in_bias, w_back, back_bias, cotangent):
    rows = tokens.shape[0]
    share = w_qkv.shape[0]
    hidden = in_bias.shape[1]
    half = hidden // 2
    planes = 2 * depth
    core = lax.axis_index("c")
    y = lax.axis_index("y")
    x = lax.axis_index("x")

    parts = [w_qkv[:, :D], w_qkv[:, D:2 * D], w_qkv[:, 2 * D:], w_out]
    mat_a = jnp.where(core == 0, parts[0], parts[2])
    mat_b = jnp.where(core == 0, parts[1], parts[3])
    small = jnp.stack([ln1_gain, ln1_bias, out_bias, ln2_gain, ln2_bias, back_bias[0], back_bias[1], back_bias[2]])
    small = jnp.pad(small, ((0, 0), (0, 128 - share)))
    small = jnp.concatenate([small, jnp.pad(in_bias, ((0, 5), (0, D - 128 - hidden)))], axis=1)
    message = jnp.concatenate([mat_a, small, mat_b], axis=0)
    cut = share + 8
    first = spread(message, depth)
    near = [first, swap(first, "x"), swap(first, "y"), diagonal(first)]
    pieces = near + [swap(piece, "c") for piece in near]
    small_x = ordered(near[0][:, share:cut], near[1][:, share:cut], x, 1)
    small_other = ordered(near[2][:, share:cut], near[3][:, share:cut], x, 1)
    rows_all = ordered(small_x, small_other, y, 1).reshape(2 * planes, 8, D)
    vec = jnp.transpose(rows_all[:, :, :share], (1, 0, 2)).reshape(8, D).astype(F32)
    bias_all = rows_all[:, :EXPERTS, 128:128 + hidden].reshape(planes, 2, EXPERTS, 2, half)
    bias_mine = lax.dynamic_index_in_dim(bias_all, x, 1, keepdims=False)
    bias_mine = lax.dynamic_index_in_dim(bias_mine, core, 2, keepdims=False)
    bias_mine = jnp.transpose(bias_mine, (1, 0, 2)).reshape(EXPERTS, 1, planes * half).astype(F32)

    hot = modality.astype(F32)
    before = jnp.arange(rows, dtype=jnp.int32)
    triangle = (before[None, :] < before[:, None]).astype(BF16)
    rank = dot(triangle, hot.astype(BF16))
    counts = jnp.sum(modality, axis=0)
    units = (counts + UNIT - 1) // UNIT
    starts = running(units, 0) - units
    place = jnp.sum(hot * (rank + (starts * UNIT).astype(F32)[None, :]), axis=1).astype(jnp.int32)
    room = rows // UNIT + EXPERTS - 1
    slots = jnp.arange(room * UNIT, dtype=jnp.int32)
    perm = (slots[:, None] == place[None, :]).astype(BF16)
    unperm = (place[:, None] == slots[None, :]).astype(BF16)
    cs = dot(perm, cotangent).astype(BF16)

    def four(value):
        beside = swap(value, "x")
        return [value, beside, swap(value, "c"), swap(beside, "c")]

    units_all = jnp.stack(four(units.astype(F32))).astype(jnp.int32)
    starts_all = running(units_all, 1) - units_all + (jnp.arange(4, dtype=jnp.int32) * room)[:, None]
    ends = running(units_all, 0)
    begins = ends - units_all
    totals = ends[3]
    index = jnp.arange(4 * rows // UNIT + UNITS, dtype=jnp.int32)[:, None, None]
    inside = (index >= begins[None]) & (index < ends[None])
    table = jnp.sum(jnp.where(inside, starts_all[None] + index - begins[None], 0), axis=1).T

    cs_all = four(after(cs, near[3]))

    columns = w_in.reshape(EXPERTS, share, planes, 2, 2, half)
    columns = lax.dynamic_index_in_dim(columns, core, 4, keepdims=False)
    in_mine, in_other = halves(columns, x, 3)
    in_mine = in_mine.reshape(EXPERTS, share, planes * half)
    in_other = in_other.reshape(EXPERTS, share, planes * half)
    in_pair = ordered(in_mine, swap(in_other, "x"), x, 1).reshape(EXPERTS, 2 * share, planes * half)
    back_mine = lax.dynamic_slice_in_dim(w_back, core * half, half, 1)
    experts = []
    wait_for = [first, near[3], None]
    for e in range(EXPERTS):
        wait = experts[0][0] if e == 2 else wait_for[e]
        block = after(jnp.concatenate([in_pair[e], back_mine[e]], axis=0), wait)
        got = spread(block, depth)
        experts.append([got, swap(got, "y")])

    where = jnp.stack([core, y, x]).astype(jnp.int32)
    middle, xs, q, k, v, mixed, probs, weights = attn_fwd(where, lengths, tokens, vec, perm, pieces, share)
    xs_all = four(xs)

    state = None
    grads, bias_grads = [], []
    for e in range(EXPERTS):
        *state, mine, other, bias_grad = ffn(
            table[e], totals[e][None], where, xs_all, cs_all, experts[e], bias_mine[e], state
        )
        bias_grads.append(bias_grad)
        grads.append((mine, other))
    used = (jnp.sum(units) * UNIT).astype(jnp.int32)

    def home(near, far):
        near = add_low(near, swap(far, "c")).reshape(2, room * UNIT, D)
        total = near[0].astype(F32) + swap(near[1], "x").astype(F32)
        return jnp.where(slots[:, None] < used, total, 0.0).astype(BF16)

    dxs = home(state[2], state[3])
    shards = []
    for mine, other in grads:
        summed = add_low(mine, swap(other, "y"))
        summed = lax.all_to_all(summed, "z", 0, 0, tiled=True)
        shards.append(jnp.sum(summed.astype(F32), axis=0))

    hot_rows = jnp.pad(jnp.transpose(modality.astype(BF16)), ((0, 5), (0, 0)))
    grad_tokens, keep, send, gvec = attn_bwd(
        where, tokens, cotangent, middle, dxs, unperm, q, k, v, mixed, probs, vec, hot_rows, weights,
    )
    outs = home(state[0], state[1])
    output = (middle + dot(unperm, outs) + dot(hot.astype(BF16), vec[5:8].astype(BF16))).astype(BF16)

    vec_msg = jnp.transpose(gvec.reshape(8, 2 * planes, share), (1, 0, 2))
    vec_msg = jnp.pad(vec_msg, ((0, 0), (0, 0), (0, 128 - share)))
    in_grad = jnp.concatenate(bias_grads, axis=0).reshape(EXPERTS, planes, half)
    in_grad = jnp.transpose(in_grad, (1, 0, 2))[:, None, :, None, :]
    in_grad = in_grad * (jnp.arange(2) == x).astype(F32)[None, :, None, None, None]
    in_grad = in_grad * (jnp.arange(2) == core).astype(F32)[None, None, None, :, None]
    in_grad = in_grad.reshape(2 * planes, EXPERTS, hidden)
    in_grad = jnp.pad(in_grad, ((0, 0), (0, 5), (0, D - 128 - hidden)))
    vec_msg = jnp.concatenate([vec_msg, in_grad], axis=2).astype(BF16)
    keep = keep.reshape(2, 2 * planes, share, D)
    got = swap(send, "c").reshape(2, 2 * planes, share, D)
    vec_sum = add_low(vec_msg, swap(vec_msg, "c"))
    part = jnp.concatenate([add_low(keep[0], got[0]), vec_sum, add_low(keep[1], got[1])], axis=1)
    part = part.reshape(depth, 2, 2, cut + share, D)
    mine_y, other_y = halves(part, y, 1)
    mine, other_x = halves(mine_y, x, 1)
    only_y, other = halves(other_y, x, 1)
    part = mine.astype(F32) + swap(other_x, "x").astype(F32) + swap(only_y, "y").astype(F32)
    part = (part + diagonal(other).astype(F32)).astype(BF16)
    done = lax.all_to_all(part, "z", 0, 0, tiled=True)
    done = jnp.sum(done.astype(F32), axis=0)
    small = done[share:cut]
    done_low = done.astype(BF16)
    pair = jnp.stack([done_low[:share], done_low[cut:]])
    away = swap(pair, "c")
    grad_q = jnp.where(core == 0, pair[0], away[0])
    grad_k = jnp.where(core == 0, pair[1], away[1])
    grad_v = jnp.where(core == 0, away[0], pair[0])
    grad_o = jnp.where(core == 0, away[1], pair[1])
    grad_w_qkv = jnp.concatenate([grad_q, grad_k, grad_v], axis=1)

    shards = jnp.stack(shards).astype(BF16)
    in_mine, in_other = halves(shards[:, :2 * share].reshape(EXPERTS, 2, share, D), x, 1)
    in_pair = ordered(in_mine, swap(in_other, "x"), x, 2)
    in_pair_c, back_c = swap(in_pair, "c"), swap(shards[:, 2 * share:], "c")
    grad_w_in = ordered(in_pair, in_pair_c, core, 3)
    grad_w_in = grad_w_in.reshape(EXPERTS, share, 2, 2, planes, half)
    grad_w_in = jnp.transpose(grad_w_in, (0, 1, 4, 2, 3, 5)).reshape(EXPERTS, share, 2 * planes * hidden)
    grad_w_back = ordered(shards[:, 2 * share:], back_c, core, 1).reshape(EXPERTS, hidden, D)

    result = (
        small[0, :share], small[1, :share], grad_w_qkv, grad_o, small[2, :share], small[3, :share], small[4, :share],
        grad_w_in, small[:EXPERTS, 128:128 + hidden], grad_w_back, small[5:8, :share],
    )
    if outer > 1:
        result = tuple(lax.psum(item.astype(BF16), "ro") for item in result)
    return (output, grad_tokens) + tuple(item.astype(F32) for item in result)


def solution(mesh):
    reps, shards = mesh.shape["rep"], mesh.shape["fsdp"]
    grid = Mesh(mesh.devices.reshape(reps // 2, 2, shards // 4, 2, 2), ("ro", "c", "z", "y", "x"))
    fsdp = ("z", "y", "x")
    every = ("ro", "c", "z", "y", "x")
    vector, matrix, stack, lines = P(fsdp), P(fsdp, None), P(None, fsdp, None), P(None, fsdp)
    placed = (
        P(every, None), P(every, None), P(every), vector, vector, matrix, matrix, vector, vector, vector,
        stack, lines, stack, lines, P(every, None),
    )
    out = (
        P(every, None), P(every, None), vector, vector, matrix, matrix, vector, vector, vector,
        stack, lines, stack, lines,
    )
    return jax.shard_map(
        functools.partial(body, reps // 2, shards // 4), mesh=grid, in_specs=placed, out_specs=out, check_vma=False
    )
```

```python
import functools
import math

import jax
import jax.numpy as jnp
from jax import lax
from jax.experimental import pallas as pl
from jax.experimental.pallas import tpu as pltpu
from jax.sharding import Mesh
from jax.sharding import PartitionSpec as P

HEADS = 12
HEAD_DIM = 64
SEQ = 256
D = 768
EXPERTS = 3
UNIT = 16
TILE = 256
UNITS = TILE // UNIT

INV_ROOT_TWO = 1.0 / math.sqrt(2.0)
INV_ROOT_TAU = 1.0 / math.sqrt(2.0 * math.pi)
F32 = jnp.float32
BF16 = jnp.bfloat16

VMEM = pl.BlockSpec(memory_space=pltpu.VMEM)
SMEM = pl.BlockSpec(memory_space=pltpu.SMEM)
ANY = pl.BlockSpec(memory_space=pl.ANY)

SMALL_LANES = 128
SMALL = pl.CostEstimate(flops=1, bytes_accessed=1, transcendentals=0)


def dot(a, b):
    return lax.dot_general(a, b, (((1,), (0,)), ((), ())), preferred_element_type=F32)


def dot_nt(a, b):
    return lax.dot_general(a, b, (((1,), (1,)), ((), ())), preferred_element_type=F32)


def dot_tn(a, b):
    return lax.dot_general(a, b, (((0,), (0,)), ((), ())), preferred_element_type=F32)


def norm_stats(values):
    average = jnp.mean(values, axis=-1, keepdims=True)
    centred = values - average
    inverse = lax.rsqrt(jnp.mean(centred * centred, axis=-1, keepdims=True) + 1e-05)
    return centred * inverse, inverse


def norm_backward(weighted, scaled, inverse):
    first = jnp.mean(weighted, axis=-1, keepdims=True)
    second = jnp.mean(weighted * scaled, axis=-1, keepdims=True)
    return inverse * (weighted - first - scaled * second)


def two_heads(block):
    low = lax.broadcasted_iota(jnp.int32, block.shape, 1) < HEAD_DIM
    nothing = jnp.zeros_like(block)
    return jnp.concatenate([jnp.where(low, block, nothing), jnp.where(low, nothing, block)], axis=0)


def merge_heads(block):
    low = lax.broadcasted_iota(jnp.int32, (SEQ, 2 * HEAD_DIM), 1) < HEAD_DIM
    return jnp.where(low, block[:SEQ], block[SEQ:])


PAIRS = HEADS // 2


def attn_fwd_kernel(share, where_ref, len_ref, place_ref, tok_ref, *rest):
    pieces = rest[:8]
    mid_ref, xs_a, xs_b, q_ref, k_ref, v_ref, mixed_ref, probs_ref, w_ref, vec_ref, bias_ref = rest[8:19]
    tok, low, sems, own_sems = rest[19:]
    fetch_tok = pltpu.make_async_copy(tok_ref, tok, own_sems.at[0])
    fetch_tok.start()
    fetch_low = [
        pltpu.make_async_copy(pieces[n].at[:, pl.ds(share, 8)], low.at[n], own_sems.at[1 + n]) for n in range(4)
    ]
    for copy in fetch_low:
        copy.start()
    core, y, x = where_ref[0], where_ref[1], where_ref[2]
    copies = ([], [])
    for matrix in range(2):
        for n, piece in enumerate(pieces):
            far, y_of, x_of = n // 4, (n // 2) % 2, n % 2
            slot = 2 * jnp.where(far == 1, 1 - core, core) + matrix
            place = 2 * jnp.where(y_of == 1, 1 - y, y) + jnp.where(x_of == 1, 1 - x, x)
            copies[matrix].append(pltpu.make_async_copy(
                piece.at[:, pl.ds(matrix * (share + 8), share)], w_ref.at[slot, :, place], sems.at[matrix, n]))
    for copy in copies[0] + copies[1]:
        copy.start()

    def weight(slot):
        return w_ref[slot].reshape(D, D)

    for copy in fetch_low:
        copy.wait()
    gather_small(share, core, y, x, low, vec_ref, bias_ref)
    fetch_tok.wait()
    values = tok[...].astype(F32)
    scaled, _ = norm_stats(values)
    normed = (scaled * vec_ref[0:1, :] + vec_ref[1:2, :]).astype(BF16)
    for copy in copies[0]:
        copy.wait()
    q_ref[...] = dot(normed, weight(0)).astype(BF16)
    v_ref[...] = dot(normed, weight(2)).astype(BF16)
    for copy in copies[1]:
        copy.wait()
    k_ref[...] = dot(normed, weight(1)).astype(BF16)
    seqs = tok_ref.shape[0] // SEQ
    for seq in range(seqs):
        length = len_ref[seq]
        rows = slice(seq * SEQ, (seq + 1) * SEQ)

        def step(pair, carry):
            cols = pl.ds(pl.multiple_of(pair * 128, 128), 128)
            both = two_heads(q_ref[rows, cols])
            scores = dot_nt(both, k_ref[rows, cols]) * (HEAD_DIM ** -0.5)
            valid = lax.broadcasted_iota(jnp.int32, scores.shape, 1) < length
            scores = jnp.where(valid, scores, -1e30)
            top = jnp.max(scores, axis=-1, keepdims=True)
            grown = jnp.exp(scores - top)
            total = jnp.sum(grown, axis=-1, keepdims=True)
            probs = (grown * (1.0 / total)).astype(BF16)
            probs_ref[seq * PAIRS + pair] = probs
            mixed_ref[rows, cols] = merge_heads(dot(probs, v_ref[rows, cols])).astype(BF16)
            return carry

        lax.fori_loop(0, PAIRS, step, 0)
    middle = tok[...].astype(F32) + dot(mixed_ref[...], weight(3)) + vec_ref[2:3, :]
    mid_ref[...] = middle
    scaled_two, _ = norm_stats(middle)
    normed_two = (scaled_two * vec_ref[3:4, :] + vec_ref[4:5, :]).astype(BF16)
    for n, target in enumerate((xs_a, xs_b)):
        slot = lax.broadcasted_iota(jnp.int32, (target.shape[0], tok.shape[0]), 0) + n * target.shape[0]
        perm = jnp.where(slot == place_ref[...], 1.0, 0.0).astype(BF16)
        target[...] = dot(perm, normed_two).astype(BF16)


def gather_small(share, core, y, x, low, vec_ref, bias_ref):
    depth = low.shape[1]
    half = D // (2 * depth)
    lane = lax.broadcasted_iota(jnp.int32, (8, D), 1)
    bias_lane = SMALL_LANES + core * half
    vec = jnp.zeros((8, D), F32)
    bias = jnp.zeros((8, D), F32)
    for n in range(4):
        place_y = 1 - y if n // 2 else y
        place_x = 1 - x if n % 2 else x
        for z in range(depth):
            rows = low[n, z].astype(F32)
            shift = (4 * z + 2 * place_y + place_x) * share
            vec += pltpu.roll(jnp.where(lane < share, rows, 0.0), shift, 1)
            if n % 2 == 0:
                mine = jnp.where((lane >= bias_lane) & (lane < bias_lane + half), rows, 0.0)
                bias += pltpu.roll(mine, lax.rem((2 * z + place_y) * half - bias_lane + D, D), 1)
    vec_ref[...] = vec
    bias_ref[...] = bias


def scatter_small(share, core, y, x, vec, bias, low):
    depth = low.shape[1]
    half = D // (2 * depth)
    lane = lax.broadcasted_iota(jnp.int32, (8, D), 1)
    bias_lane = SMALL_LANES + core * half
    for n in range(4):
        place_y = 1 - y if n // 2 else y
        place_x = 1 - x if n % 2 else x
        for z in range(depth):
            shift = (4 * z + 2 * place_y + place_x) * share
            rows = jnp.where(lane < share, pltpu.roll(vec, lax.rem(D - shift, D), 1), 0.0)
            if n % 2 == 0:
                mine = pltpu.roll(bias, lax.rem(bias_lane - (2 * z + place_y) * half + D, D), 1)
                rows += jnp.where((lane >= bias_lane) & (lane < bias_lane + half), mine, 0.0)
            low[n, z] = rows.astype(BF16)


def attn_fwd(where, lengths, place, tokens, pieces, share, room):
    rows = tokens.shape[0]
    seqs = rows // SEQ
    low = jax.ShapeDtypeStruct((rows, D), BF16)
    return pl.pallas_call(
        functools.partial(attn_fwd_kernel, share),
        out_shape=(
            jax.ShapeDtypeStruct((rows, D), F32),
            jax.ShapeDtypeStruct((room * UNIT // 2, D), BF16),
            jax.ShapeDtypeStruct((room * UNIT // 2, D), BF16),
            low, low, low, low,
            jax.ShapeDtypeStruct((seqs * PAIRS, 2 * SEQ, SEQ), BF16),
            jax.ShapeDtypeStruct((4, pieces[0].shape[0], 4, share, D), BF16),
            jax.ShapeDtypeStruct((8, D), F32),
            jax.ShapeDtypeStruct((8, D), F32),
        ),
        in_specs=[SMEM] * 2 + [VMEM] + [ANY] * 9,
        out_specs=(VMEM,) * 11,
        scratch_shapes=[
            pltpu.VMEM(tokens.shape, BF16),
            pltpu.VMEM((4, pieces[0].shape[0], 8, D), BF16),
            pltpu.SemaphoreType.DMA((2, 8)),
            pltpu.SemaphoreType.DMA((5,)),
        ],
        compiler_params=pltpu.CompilerParams(vmem_limit_bytes=60 * 1024 * 1024),
        cost_estimate=pl.CostEstimate(flops=6 * 10**9, bytes_accessed=1, transcendentals=0),
        name="attn_fwd",
    )(where, lengths, place, tokens, *pieces)


def ffn_kernel(e, first, count, whole, tab_ref, tot_ref, where_ref, *rest):
    xs, cs, ws, b_ref = rest[0:8], rest[8:12], rest[12:12 + count], rest[12 + count]
    rest = rest[13 + count:] if first else rest[25 + count:]
    outs, mine_ref, other_ref, gb_ref = rest[:12], rest[12], rest[-15], rest[-14]
    xv, cv, wi, wb, gwi, gwb, xt, ct, ot, dt, in_sems, w_sems, out_sems = rest[-13:]
    y = where_ref[1]
    height = mine_ref.shape[1] // 2
    depth = D // height // 2
    size = cs[0].shape[0]
    weights, tokens = [], []
    for part, target in enumerate((wi, wb)):
        held = pl.ds(part * height, height)
        for n, piece in enumerate(ws):
            place = target if count == 1 else target.at[:, y if n == 0 else 1 - y]
            weights.append(pltpu.make_async_copy(piece.at[:, held], place, w_sems.at[n, part]))
    for n in range(8):
        part = pl.ds(n * (size // 2), size // 2)
        tokens.append(pltpu.make_async_copy(xs[n], xv.at[part], in_sems.at[0, n]))
    for n in range(4):
        tokens.append(pltpu.make_async_copy(cs[n], cv.at[pl.ds(n * size, size)], in_sems.at[1, n]))
    for copy in tokens + weights:
        copy.start()
    gwi[...] = jnp.zeros_like(gwi)
    gwb[...] = jnp.zeros_like(gwb)
    gb_ref[...] = jnp.zeros_like(gb_ref)
    for copy in tokens + weights:
        copy.wait()
    total = tot_ref[0]
    room = size // UNIT

    def pick(low, high, value, found):
        if high - low == 1:
            found(low)
            return
        middle = (low + high) // 2
        lax.cond(
            value < middle, lambda: pick(low, middle, value, found), lambda: pick(middle, high, value, found)
        )

    def send(t, u):
        unit = t * UNITS + u
        held = slice(u * UNIT, (u + 1) * UNIT)

        @pl.when(unit < total)
        def _():
            dst = tab_ref[unit]
            half_of = lax.div(2 * dst, room)

            def found(n):
                for m, (tile_ref, target, first_unit) in enumerate(
                    ((ot, outs[n // 2], n // 2 * room), (dt, outs[4 + n], n * (room // 2)))
                ):
                    rows = pl.ds(pl.multiple_of((dst - first_unit) * UNIT, UNIT), UNIT)
                    pltpu.make_async_copy(tile_ref.at[held], target.at[rows], out_sems.at[m, u]).start()

            pick(0, 8, half_of, found)

    def settle(t, u):
        @pl.when(t * UNITS + u < total)
        def _():
            held = slice(u * UNIT, (u + 1) * UNIT)
            for m, (tile_ref, target) in enumerate(((ot, outs[0]), (dt, outs[4]))):
                pltpu.make_async_copy(tile_ref.at[held], target.at[pl.ds(0, UNIT)], out_sems.at[m, u]).wait()

    def tile(t, carry):
        for u in range(UNITS):
            src = pl.multiple_of(tab_ref[t * UNITS + u] * UNIT, UNIT)
            xt[u * UNIT:(u + 1) * UNIT, :] = xv[pl.ds(src, UNIT), :]
            ct[u * UNIT:(u + 1) * UNIT, :] = cv[pl.ds(src, UNIT), :]
        left = (total - t * UNITS) * UNIT
        row = lax.broadcasted_iota(jnp.int32, (TILE, D), 0)
        part = jnp.where(row < left, ct[...], jnp.zeros_like(ct))
        pre = dot(xt[...], wi[...].reshape(D, -1)) + b_ref[e:e + 1, :]
        share = 0.5 * (1.0 + lax.erf(pre * INV_ROOT_TWO))
        act = (pre * share).astype(BF16)
        slope = share + pre * jnp.exp(-0.5 * pre * pre) * INV_ROOT_TAU

        @pl.when(t > 0)
        def _():
            for u in range(UNITS):
                settle(t - 1, u)

        ot[...] = dot(act, wb[...].reshape(-1, D)).astype(BF16)
        pre_grad = (dot_nt(part, wb[...].reshape(-1, D)) * slope).astype(BF16)
        dt[...] = dot_nt(pre_grad, wi[...].reshape(D, -1)).astype(BF16)
        for u in range(UNITS):
            send(t, u)
        gwb[...] += dot_tn(act, part)
        gwi[...] += dot_tn(xt[...], pre_grad)
        gb_ref[...] += jnp.sum(pre_grad.astype(F32), axis=0, keepdims=True)
        return carry

    tiles = (total + UNITS - 1) // UNITS
    lax.fori_loop(0, tiles, tile, 0)

    @pl.when(tiles > 0)
    def _():
        for u in range(UNITS):
            settle(tiles - 1, u)

    if whole:
        for b in range(2 * depth):
            mine_ref[b, :height, :] = gwi[b * height:(b + 1) * height, :].astype(BF16)
            mine_ref[b, height:, :] = gwb[b * height:(b + 1) * height, :].astype(BF16)
        return
    for z in range(depth):
        for y_of in range(2):
            rows = slice((2 * z + y_of) * height, (2 * z + y_of + 1) * height)
            for flag, target in ((y == y_of, mine_ref), (y != y_of, other_ref)):
                @pl.when(flag)
                def _():
                    target[z, :height, :] = gwi[rows, :].astype(BF16)
                    target[z, height:, :] = gwb[rows, :].astype(BF16)


def ffn(e, table, total, where, xs, cs, weights, bias, before, whole):
    size = cs[0].shape[0]
    first = before is None
    quarter = bias.shape[1]
    tokens = [jax.ShapeDtypeStruct((size, D), BF16)] * 4 + [jax.ShapeDtypeStruct((size // 2, D), BF16)] * 8
    height = weights[0].shape[-2] // 2
    blocked = (D // height, height, D) if len(weights) == 1 else (D // height // 2, 2, height, D)
    blocks = D // height
    grads = [jax.ShapeDtypeStruct((blocks if whole else blocks // 2, 2 * height, D), BF16)] * (1 if whole else 2)
    args = [table, total, where, *xs, *cs, *weights, bias] + ([] if first else list(before))
    return pl.pallas_call(
        functools.partial(ffn_kernel, e, first, len(weights), whole),
        out_shape=(*tokens, *grads, jax.ShapeDtypeStruct((1, quarter), F32)),
        in_specs=[SMEM] * 3 + [ANY] * (12 + len(weights)) + [VMEM] + [ANY] * (0 if first else 12),
        out_specs=(ANY,) * 12 + (VMEM,) * (1 + len(grads)),
        scratch_shapes=[
            pltpu.VMEM((4 * size, D), BF16),
            pltpu.VMEM((4 * size, D), BF16),
            pltpu.VMEM(blocked, BF16),
            pltpu.VMEM(blocked, BF16),
            pltpu.VMEM((D, quarter), F32),
            pltpu.VMEM((quarter, D), F32),
            pltpu.VMEM((TILE, D), BF16),
            pltpu.VMEM((TILE, D), BF16),
            pltpu.VMEM((TILE, D), BF16),
            pltpu.VMEM((TILE, D), BF16),
            pltpu.SemaphoreType.DMA((2, 8)),
            pltpu.SemaphoreType.DMA((len(weights), 2)),
            pltpu.SemaphoreType.DMA((2, UNITS)),
        ],
        input_output_aliases={} if first else {16 + len(weights) + i: i for i in range(12)},
        compiler_params=pltpu.CompilerParams(vmem_limit_bytes=60 * 1024 * 1024),
        cost_estimate=SMALL,
        name="ffn",
    )(*args)


def attn_bwd_kernel(share, where_ref, vec_ref, hot_ref, place_ref, bias_a, bias_b, bias_c, *rest):
    far, outs, held = rest[:11], rest[11:20], rest[20:31]
    gtok_ref, keeps, sends = outs[0], outs[1:5], outs[5:9]
    mg, mxg, dq, dk, dv, gw, gvec_ref, small, sems, out_sems = rest[31:]
    core, y, x = where_ref[0], where_ref[1], where_ref[2]
    leaving = []
    copies = [pltpu.make_async_copy(a, b, sems.at[n]) for n, (a, b) in enumerate(zip(far, held))]
    for copy in copies:
        copy.start()
    dx_a, dx_b, mid, cot, mixed, w_ref, q_ref, k_ref, v_ref, probs_ref, tok = held
    slot = lax.broadcasted_iota(jnp.int32, (tok.shape[0], 2 * dx_a.shape[0]), 1)
    unperm = jnp.where(slot == place_ref[...], 1.0, 0.0).astype(BF16)
    for copy in copies[:4]:
        copy.wait()
    norm2_grad = dot(unperm, jnp.concatenate([dx_a[...], dx_b[...]], axis=0))
    scaled_two, inverse_two = norm_stats(mid[...])
    gvec_ref[3:4, :] = jnp.sum(norm2_grad * scaled_two, axis=0, keepdims=True)
    gvec_ref[4:5, :] = jnp.sum(norm2_grad, axis=0, keepdims=True)
    mid_grad = cot[...].astype(F32) + norm_backward(norm2_grad * vec_ref[3:4, :], scaled_two, inverse_two)
    mg[...] = mid_grad
    branch = mid_grad.astype(BF16)
    gvec_ref[2:3, :] = jnp.sum(branch.astype(F32), axis=0, keepdims=True)
    gvec_ref[5:8, :] = dot(hot_ref[...], cot[...])[:3]
    for copy in copies[4:6]:
        copy.wait()

    def put(matrix, value):
        gw[matrix] = value.astype(BF16).reshape(gw.shape[1:])
        rows = pl.ds((matrix % 2) * (share + 8), share)
        for n in range(4):
            place = 2 * (1 - y if n // 2 else y) + (1 - x if n % 2 else x)
            for flag, target in ((core == matrix // 2, keeps[n]), (core != matrix // 2, sends[n])):
                def copy(target=target, place=place, n=n):
                    return pltpu.make_async_copy(gw.at[matrix, :, place], target.at[:, rows], out_sems.at[matrix, n])

                pl.when(flag)(lambda: copy().start())
                leaving.append((flag, copy))

    put(3, dot_tn(mixed[...], branch))
    mxg[...] = dot_nt(branch, w_ref[3].reshape(D, D)).astype(BF16)
    for copy in copies[6:]:
        copy.wait()
    seqs = tok.shape[0] // SEQ
    scale = HEAD_DIM ** -0.5
    for seq in range(seqs):
        rows = slice(seq * SEQ, (seq + 1) * SEQ)

        def step(pair, carry):
            cols = pl.ds(pl.multiple_of(pair * 128, 128), 128)
            probs = probs_ref[seq * PAIRS + pair]
            grads = two_heads(mxg[rows, cols])
            dv[rows, cols] = dot_tn(probs, grads).astype(BF16)
            prob_grad = dot_nt(grads, v_ref[rows, cols])
            wide = probs.astype(F32)
            inner = jnp.sum(wide * prob_grad, axis=-1, keepdims=True)
            score_grad = (wide * (prob_grad - inner)).astype(BF16)
            dq[rows, cols] = (merge_heads(dot(score_grad, k_ref[rows, cols])) * scale).astype(BF16)
            dk[rows, cols] = (dot_tn(score_grad, two_heads(q_ref[rows, cols])) * scale).astype(BF16)
            return carry

        lax.fori_loop(0, PAIRS, step, 0)
    scaled, inverse = norm_stats(tok[...].astype(F32))
    normed = (scaled * vec_ref[0:1, :] + vec_ref[1:2, :]).astype(BF16)
    put(0, dot_tn(normed, dq[...]))
    put(1, dot_tn(normed, dk[...]))
    put(2, dot_tn(normed, dv[...]))
    norm1_grad = dot_nt(dq[...], w_ref[0].reshape(D, D)) + dot_nt(dk[...], w_ref[1].reshape(D, D)) + dot_nt(dv[...], w_ref[2].reshape(D, D))
    gvec_ref[0:1, :] = jnp.sum(norm1_grad * scaled, axis=0, keepdims=True)
    gvec_ref[1:2, :] = jnp.sum(norm1_grad, axis=0, keepdims=True)
    bias = jnp.concatenate([bias_a[...], bias_b[...], bias_c[...], jnp.zeros((5, D), F32)], axis=0)
    scatter_small(share, core, y, x, gvec_ref[...], bias, small)
    for n in range(4):
        for m, target in enumerate((keeps[n], sends[n])):
            copy = pltpu.make_async_copy(small.at[n], target.at[:, pl.ds(share, 8)], out_sems.at[4 + m, n])
            copy.start()
            leaving.append((None, copy))
    gtok_ref[...] = (mg[...] + norm_backward(norm1_grad * vec_ref[0:1, :], scaled, inverse)).astype(BF16)
    for flag, copy in leaving:
        if flag is None:
            copy.wait()
        else:
            pl.when(flag)(lambda copy=copy: copy().wait())


def attn_bwd(share, where, vec, hot, place, bias_grads, far):
    rows = far[-1].shape[0]
    depth = D // share // 4
    part = jax.ShapeDtypeStruct((depth, 2 * share + 8, D), BF16)
    return pl.pallas_call(
        functools.partial(attn_bwd_kernel, share),
        out_shape=(jax.ShapeDtypeStruct((rows, D), BF16),) + (part,) * 8,
        in_specs=[SMEM] + [VMEM] * 6 + [ANY] * 11,
        out_specs=(VMEM,) + (ANY,) * 8,
        scratch_shapes=[pltpu.VMEM(item.shape, item.dtype) for item in far]
        + [pltpu.VMEM((rows, D), F32)] + [pltpu.VMEM((rows, D), BF16)] * 4
        + [
            pltpu.VMEM((4, depth, 4, share, D), BF16),
            pltpu.VMEM((8, D), F32),
            pltpu.VMEM((4, depth, 8, D), BF16),
            pltpu.SemaphoreType.DMA((11,)),
            pltpu.SemaphoreType.DMA((6, 4)),
        ],
        compiler_params=pltpu.CompilerParams(vmem_limit_bytes=60 * 1024 * 1024),
        cost_estimate=SMALL,
        name="attn_bwd",
    )(where, vec, hot, place, *bias_grads, *far)


def swap(value, axis):
    return lax.ppermute(value, axis, [(0, 1), (1, 0)])


def diagonal(value):
    return lax.ppermute(value, ("y", "x"), [(i, 3 - i) for i in range(4)])


def after_kernel(*refs):
    pass


def after(value, *others):
    return pl.pallas_call(
        after_kernel,
        out_shape=jax.ShapeDtypeStruct(value.shape, value.dtype),
        in_specs=[ANY] * (1 + len(others)),
        out_specs=ANY,
        input_output_aliases={0: 0},
        cost_estimate=SMALL,
        name="after",
    )(value, *others)


def ordered(mine, other, index, axis):
    first = jnp.where(index == 0, mine, other)
    second = jnp.where(index == 0, other, mine)
    return jnp.stack([first, second], axis=axis)


def spread(block, count, *wait):
    copies = jnp.broadcast_to(block[None], (count,) + block.shape)
    return lax.all_to_all(after(copies, *wait) if wait else copies, "z", 0, 0, tiled=True)


def halves(value, index, axis):
    mine = lax.dynamic_index_in_dim(value, index, axis, keepdims=False)
    other = lax.dynamic_index_in_dim(value, 1 - index, axis, keepdims=False)
    return mine, other


def running(values, axis):
    steps = [lax.index_in_dim(values, 0, axis, keepdims=False)]
    for i in range(1, values.shape[axis]):
        steps.append(steps[-1] + lax.index_in_dim(values, i, axis, keepdims=False))
    return jnp.stack(steps, axis=axis)


def add_low(a, b):
    return (a.astype(F32) + b.astype(F32)).astype(BF16)


def body(outer, depth, tokens, modality, lengths, ln1_gain, ln1_bias, w_qkv, w_out, out_bias, ln2_gain, ln2_bias,
         w_in, in_bias, w_back, back_bias, cotangent):
    rows = tokens.shape[0]
    share = w_qkv.shape[0]
    hidden = in_bias.shape[1]
    half = hidden // 2
    planes = 2 * depth
    core = lax.axis_index("c")
    y = lax.axis_index("y")
    x = lax.axis_index("x")

    hot = modality.astype(F32)
    before = jnp.arange(rows, dtype=jnp.int32)
    triangle = (before[None, :] < before[:, None]).astype(BF16)
    rank = dot(triangle, hot.astype(BF16))
    counts = jnp.sum(modality, axis=0)
    units = (counts + UNIT - 1) // UNIT
    starts = running(units, 0) - units
    place = jnp.sum(hot * (rank + (starts * UNIT).astype(F32)[None, :]), axis=1).astype(jnp.int32)
    room = rows // UNIT + EXPERTS - 1
    slots = jnp.arange(room * UNIT, dtype=jnp.int32)
    perm = (slots[:, None] == place[None, :]).astype(BF16)
    unperm = (place[:, None] == slots[None, :]).astype(BF16)
    cs = dot(perm, cotangent).astype(BF16)

    parts = [w_qkv[:, :D], w_qkv[:, D:2 * D], w_qkv[:, 2 * D:], w_out]
    mat_a = jnp.where(core == 0, parts[0], parts[2])
    mat_b = jnp.where(core == 0, parts[1], parts[3])
    small = jnp.stack([ln1_gain, ln1_bias, out_bias, ln2_gain, ln2_bias, back_bias[0], back_bias[1], back_bias[2]])
    small = jnp.pad(small, ((0, 0), (0, SMALL_LANES - share)))
    small = jnp.concatenate([small, jnp.pad(in_bias, ((0, 5), (0, D - SMALL_LANES - hidden)))], axis=1)
    message = jnp.concatenate([mat_a, small, mat_b], axis=0)
    cut = share + 8
    first = after(spread(message, depth), cs)
    near = [first, swap(first, "x"), swap(first, "y"), diagonal(first)]
    pieces = near + [swap(piece, "c") for piece in near]
    def four(value):
        beside = swap(value, "x")
        return [value, beside, swap(value, "c"), swap(beside, "c")]

    units_all = jnp.stack(four(units.astype(F32))).astype(jnp.int32)
    starts_all = running(units_all, 1) - units_all + (jnp.arange(4, dtype=jnp.int32) * room)[:, None]
    ends = running(units_all, 0)
    begins = ends - units_all
    totals = ends[3]
    index = jnp.arange(4 * rows // UNIT + UNITS, dtype=jnp.int32)[:, None, None]
    inside = (index >= begins[None]) & (index < ends[None])
    table = jnp.sum(jnp.where(inside, starts_all[None] + index - begins[None], 0), axis=1).T

    cs_all = four(after(cs, near[3]))

    columns = w_in.reshape(EXPERTS, share, planes, 2, 2, half)
    columns = lax.dynamic_index_in_dim(columns, core, 4, keepdims=False)
    in_mine, in_other = halves(columns, x, 3)
    in_mine = in_mine.reshape(EXPERTS, share, planes * half)
    in_other = in_other.reshape(EXPERTS, share, planes * half)
    in_pair = ordered(in_mine, swap(in_other, "x"), x, 1).reshape(EXPERTS, 2 * share, planes * half)
    back_mine = lax.dynamic_slice_in_dim(w_back, core * half, half, 1)
    block = [jnp.concatenate([in_pair[e], back_mine[e]], axis=0) for e in range(EXPERTS)]
    blocks = (planes, 2 * share + half, D)
    beside = swap(jnp.concatenate([in_mine[2], back_mine[2]], axis=0), "y")
    beside_in = ordered(beside[:share], diagonal(in_other[2]), x, 0).reshape(2 * share, planes * half)
    beside = jnp.concatenate([beside_in, beside[share:]], axis=0)
    first_in = spread(block[0], depth, pieces[4])
    second_in = spread(block[1], depth, *near[1:])
    third = lax.all_gather(after(ordered(block[2], beside, y, 0), *near[1:]), "z", axis=0).reshape(blocks)

    where = jnp.stack([core, y, x]).astype(jnp.int32)
    middle, *xs, q, k, v, mixed, probs, weights, vec, bias_mine = attn_fwd(
        where, lengths, after(place[None, :], first_in), tokens, pieces, share, room
    )
    xs_all = [item for pair in zip(*(four(part) for part in xs)) for item in pair]

    state = None
    grads, bias_grads = [None] * EXPERTS, [None] * EXPERTS
    second_in = after(second_in, xs_all[2])
    experts = [[first_in, swap(first_in, "y")], [second_in, swap(second_in, "y")], [third]]
    for e in range(EXPERTS):
        *results, bias_grads[e] = ffn(
            e, table[e], totals[e][None], where, xs_all, cs_all, experts[e], bias_mine, state, e != 2
        )
        state, grads[e] = results[:12], results[12:]
    used = (jnp.sum(units) * UNIT).astype(jnp.int32)

    def pair_sums(own, beside, across, corner):
        beside = add_low(beside, swap(corner, "c"))
        return add_low(own, swap(across, "c")), beside

    def home(own, beside, first=0):
        total = own.astype(F32) + swap(beside, "x").astype(F32)
        line = slots[first:first + own.shape[0], None]
        return jnp.where(line < used, total, 0.0).astype(BF16)

    def scatter_z(parts):
        return lax.all_to_all(parts.reshape(depth, -1, D), "z", 0, 0, tiled=True)

    last = scatter_z(grads[1][0])
    other_sum = swap(grads[2][1], "y")
    shard_low = lax.psum_scatter(grads[0][0], ("z", "y"), scatter_dimension=0)
    dx_pairs = [pair_sums(*state[4 + part::2]) for part in range(2)]
    out_pair = pair_sums(*state[:4])
    dxs = [home(*pair, part * room * UNIT // 2) for part, pair in enumerate(dx_pairs)]
    dxs[0] = after(dxs[0], *out_pair)

    hot_rows = jnp.pad(jnp.transpose(modality.astype(BF16)), ((0, 5), (0, 0)))
    grad_tokens, *parts = attn_bwd(
        share, where, vec, hot_rows, place[:, None], bias_grads,
        (*dxs, middle, cotangent, mixed, weights, q, k, v, probs, tokens),
    )
    outs = home(*out_pair)
    output = (middle + dot(unperm, outs) + dot(hot.astype(BF16), vec[5:8].astype(BF16))).astype(BF16)

    summed = [add_low(parts[n], swap(parts[4 + n], "c")) for n in (3, 1, 2, 0)]
    summed[0] = after(summed[0], shard_low)
    moved = [diagonal(summed[0]), swap(summed[1], "x"), swap(summed[2], "y"), summed[3]]
    part = (moved[0].astype(F32) + moved[1].astype(F32) + moved[2].astype(F32) + moved[3].astype(F32)).astype(BF16)
    last = jnp.sum(after(last, summed[3]).astype(F32), axis=0).reshape(2, -1, D)
    mine, other = halves(last, y, 0)
    last = mine + swap(other.astype(BF16), "y").astype(F32)
    other_sum = scatter_z(add_low(after(grads[2][0], grad_tokens), other_sum))
    shards = [shard_low.astype(F32), last, jnp.sum(other_sum.astype(F32), axis=0)]
    done = lax.all_to_all(part, "z", 0, 0, tiled=True)
    done = jnp.sum(done.astype(F32), axis=0)
    small = done[share:cut]
    done_low = done.astype(BF16)
    pair = jnp.stack([done_low[:share], done_low[cut:]])
    away = swap(pair, "c")
    grad_q = jnp.where(core == 0, pair[0], away[0])
    grad_k = jnp.where(core == 0, pair[1], away[1])
    grad_v = jnp.where(core == 0, away[0], pair[0])
    grad_o = jnp.where(core == 0, away[1], pair[1])
    grad_w_qkv = jnp.concatenate([grad_q, grad_k, grad_v], axis=1)

    shards = jnp.stack(shards).astype(BF16)
    in_mine, in_other = halves(shards[:, :2 * share].reshape(EXPERTS, 2, share, D), x, 1)
    in_pair = ordered(in_mine, swap(in_other, "x"), x, 2)
    in_pair_c, back_c = swap(in_pair, "c"), swap(shards[:, 2 * share:], "c")
    grad_w_in = ordered(in_pair, in_pair_c, core, 3)
    grad_w_in = grad_w_in.reshape(EXPERTS, share, 2, 2, planes, half)
    grad_w_in = jnp.transpose(grad_w_in, (0, 1, 4, 2, 3, 5)).reshape(EXPERTS, share, 2 * planes * hidden)
    grad_w_back = ordered(shards[:, 2 * share:], back_c, core, 1).reshape(EXPERTS, hidden, D)

    result = (
        small[0, :share], small[1, :share], grad_w_qkv, grad_o, small[2, :share], small[3, :share], small[4, :share],
        grad_w_in, small[:EXPERTS, SMALL_LANES:SMALL_LANES + hidden], grad_w_back, small[5:8, :share],
    )
    if outer > 1:
        result = tuple(lax.psum(item.astype(BF16), "ro") for item in result)
    return (output, grad_tokens) + tuple(item.astype(F32) for item in result)


def solution(mesh):
    reps, shards = mesh.shape["rep"], mesh.shape["fsdp"]
    grid = Mesh(mesh.devices.reshape(reps // 2, 2, shards // 4, 2, 2), ("ro", "c", "z", "y", "x"))
    fsdp = ("z", "y", "x")
    every = ("ro", "c", "z", "y", "x")
    vector, matrix, stack, lines = P(fsdp), P(fsdp, None), P(None, fsdp, None), P(None, fsdp)
    placed = (
        P(every, None), P(every, None), P(every), vector, vector, matrix, matrix, vector, vector, vector,
        stack, lines, stack, lines, P(every, None),
    )
    out = (
        P(every, None), P(every, None), vector, vector, matrix, matrix, vector, vector, vector,
        stack, lines, stack, lines,
    )
    return jax.shard_map(
        functools.partial(body, reps // 2, shards // 4), mesh=grid, in_specs=placed, out_specs=out, check_vma=False
    )
```

```python
import functools
import math

import jax
import jax.numpy as jnp
from jax import lax
from jax.experimental import pallas as pl
from jax.experimental.pallas import tpu as pltpu
from jax.sharding import Mesh
from jax.sharding import PartitionSpec as P

HEADS = 12
HEAD_DIM = 64
SEQ = 256
D = 768
EXPERTS = 3
UNIT = 16
TILE = 256
UNITS = TILE // UNIT

INV_ROOT_TWO = 1.0 / math.sqrt(2.0)
INV_ROOT_TAU = 1.0 / math.sqrt(2.0 * math.pi)
F32 = jnp.float32
BF16 = jnp.bfloat16

VMEM = pl.BlockSpec(memory_space=pltpu.VMEM)
SMEM = pl.BlockSpec(memory_space=pltpu.SMEM)
ANY = pl.BlockSpec(memory_space=pl.ANY)

SMALL_LANES = 128
SMALL = pl.CostEstimate(flops=1, bytes_accessed=1, transcendentals=0)


def dot(a, b):
    return lax.dot_general(a, b, (((1,), (0,)), ((), ())), preferred_element_type=F32)


def dot_nt(a, b):
    return lax.dot_general(a, b, (((1,), (1,)), ((), ())), preferred_element_type=F32)


def dot_tn(a, b):
    return lax.dot_general(a, b, (((0,), (0,)), ((), ())), preferred_element_type=F32)


def norm_stats(values):
    average = jnp.mean(values, axis=-1, keepdims=True)
    centred = values - average
    inverse = lax.rsqrt(jnp.mean(centred * centred, axis=-1, keepdims=True) + 1e-05)
    return centred * inverse, inverse


def norm_backward(weighted, scaled, inverse):
    first = jnp.mean(weighted, axis=-1, keepdims=True)
    second = jnp.mean(weighted * scaled, axis=-1, keepdims=True)
    return inverse * (weighted - first - scaled * second)


def two_heads(block):
    low = lax.broadcasted_iota(jnp.int32, block.shape, 1) < HEAD_DIM
    nothing = jnp.zeros_like(block)
    return jnp.concatenate([jnp.where(low, block, nothing), jnp.where(low, nothing, block)], axis=0)


def merge_heads(block):
    low = lax.broadcasted_iota(jnp.int32, (SEQ, 2 * HEAD_DIM), 1) < HEAD_DIM
    return jnp.where(low, block[:SEQ], block[SEQ:])


PAIRS = HEADS // 2


def attn_fwd_kernel(share, where_ref, len_ref, place_ref, tok_ref, *rest):
    pieces = rest[:8]
    mid_ref, xs_a, xs_b, q_ref, k_ref, v_ref, mixed_ref, probs_ref, w_ref, vec_ref, bias_ref = rest[8:19]
    tok, low, sems, own_sems = rest[19:]
    fetch_tok = pltpu.make_async_copy(tok_ref, tok, own_sems.at[0])
    fetch_tok.start()
    fetch_low = [
        pltpu.make_async_copy(pieces[n].at[:, pl.ds(share, 8)], low.at[n], own_sems.at[1 + n]) for n in range(4)
    ]
    for copy in fetch_low:
        copy.start()
    core, y, x = where_ref[0], where_ref[1], where_ref[2]
    copies = ([], [])
    for matrix in range(2):
        for n, piece in enumerate(pieces):
            far, y_of, x_of = n // 4, (n // 2) % 2, n % 2
            slot = 2 * jnp.where(far == 1, 1 - core, core) + matrix
            place = 2 * jnp.where(y_of == 1, 1 - y, y) + jnp.where(x_of == 1, 1 - x, x)
            copies[matrix].append(pltpu.make_async_copy(
                piece.at[:, pl.ds(matrix * (share + 8), share)], w_ref.at[slot, :, place], sems.at[matrix, n]))
    for copy in copies[0] + copies[1]:
        copy.start()

    def weight(slot):
        return w_ref[slot].reshape(D, D)

    for copy in fetch_low:
        copy.wait()
    gather_small(share, core, y, x, low, vec_ref, bias_ref)
    fetch_tok.wait()
    values = tok[...].astype(F32)
    scaled, _ = norm_stats(values)
    normed = (scaled * vec_ref[0:1, :] + vec_ref[1:2, :]).astype(BF16)
    for copy in copies[0]:
        copy.wait()
    q_ref[...] = dot(normed, weight(0)).astype(BF16)
    v_ref[...] = dot(normed, weight(2)).astype(BF16)
    for copy in copies[1]:
        copy.wait()
    k_ref[...] = dot(normed, weight(1)).astype(BF16)
    seqs = tok_ref.shape[0] // SEQ
    for seq in range(seqs):
        length = len_ref[seq]
        rows = slice(seq * SEQ, (seq + 1) * SEQ)

        def step(pair, carry):
            cols = pl.ds(pl.multiple_of(pair * 128, 128), 128)
            both = two_heads(q_ref[rows, cols])
            scores = dot_nt(both, k_ref[rows, cols]) * (HEAD_DIM ** -0.5)
            valid = lax.broadcasted_iota(jnp.int32, scores.shape, 1) < length
            scores = jnp.where(valid, scores, -1e30)
            top = jnp.max(scores, axis=-1, keepdims=True)
            grown = jnp.exp(scores - top)
            total = jnp.sum(grown, axis=-1, keepdims=True)
            probs = (grown * (1.0 / total)).astype(BF16)
            probs_ref[seq * PAIRS + pair] = probs
            mixed_ref[rows, cols] = merge_heads(dot(probs, v_ref[rows, cols])).astype(BF16)
            return carry

        lax.fori_loop(0, PAIRS, step, 0, unroll=3)
    middle = tok[...].astype(F32) + dot(mixed_ref[...], weight(3)) + vec_ref[2:3, :]
    mid_ref[...] = middle
    scaled_two, _ = norm_stats(middle)
    normed_two = (scaled_two * vec_ref[3:4, :] + vec_ref[4:5, :]).astype(BF16)
    for n, target in enumerate((xs_a, xs_b)):
        slot = lax.broadcasted_iota(jnp.int32, (target.shape[0], tok.shape[0]), 0) + n * target.shape[0]
        perm = jnp.where(slot == place_ref[...], 1.0, 0.0).astype(BF16)
        target[...] = dot(perm, normed_two).astype(BF16)


def gather_small(share, core, y, x, low, vec_ref, bias_ref):
    depth = low.shape[1]
    half = D // (2 * depth)
    lane = lax.broadcasted_iota(jnp.int32, (8, D), 1)
    bias_lane = SMALL_LANES + core * half
    vec = jnp.zeros((8, D), F32)
    bias = jnp.zeros((8, D), F32)
    for n in range(4):
        place_y = 1 - y if n // 2 else y
        place_x = 1 - x if n % 2 else x
        for z in range(depth):
            rows = low[n, z].astype(F32)
            shift = (4 * z + 2 * place_y + place_x) * share
            vec += pltpu.roll(jnp.where(lane < share, rows, 0.0), shift, 1)
            if n % 2 == 0:
                mine = jnp.where((lane >= bias_lane) & (lane < bias_lane + half), rows, 0.0)
                bias += pltpu.roll(mine, lax.rem((2 * z + place_y) * half - bias_lane + D, D), 1)
    vec_ref[...] = vec
    bias_ref[...] = bias


def scatter_small(share, core, y, x, vec, bias, low):
    depth = low.shape[1]
    half = D // (2 * depth)
    lane = lax.broadcasted_iota(jnp.int32, (8, D), 1)
    bias_lane = SMALL_LANES + core * half
    for n in range(4):
        place_y = 1 - y if n // 2 else y
        place_x = 1 - x if n % 2 else x
        for z in range(depth):
            shift = (4 * z + 2 * place_y + place_x) * share
            rows = jnp.where(lane < share, pltpu.roll(vec, lax.rem(D - shift, D), 1), 0.0)
            if n % 2 == 0:
                mine = pltpu.roll(bias, lax.rem(bias_lane - (2 * z + place_y) * half + D, D), 1)
                rows += jnp.where((lane >= bias_lane) & (lane < bias_lane + half), mine, 0.0)
            low[n, z] = rows.astype(BF16)


def attn_fwd(where, lengths, place, tokens, pieces, share, room):
    rows = tokens.shape[0]
    seqs = rows // SEQ
    low = jax.ShapeDtypeStruct((rows, D), BF16)
    return pl.pallas_call(
        functools.partial(attn_fwd_kernel, share),
        out_shape=(
            jax.ShapeDtypeStruct((rows, D), F32),
            jax.ShapeDtypeStruct((room * UNIT // 2, D), BF16),
            jax.ShapeDtypeStruct((room * UNIT // 2, D), BF16),
            low, low, low, low,
            jax.ShapeDtypeStruct((seqs * PAIRS, 2 * SEQ, SEQ), BF16),
            jax.ShapeDtypeStruct((4, pieces[0].shape[0], 4, share, D), BF16),
            jax.ShapeDtypeStruct((8, D), F32),
            jax.ShapeDtypeStruct((8, D), F32),
        ),
        in_specs=[SMEM] * 2 + [VMEM] + [ANY] * 9,
        out_specs=(VMEM,) * 11,
        scratch_shapes=[
            pltpu.VMEM(tokens.shape, BF16),
            pltpu.VMEM((4, pieces[0].shape[0], 8, D), BF16),
            pltpu.SemaphoreType.DMA((2, 8)),
            pltpu.SemaphoreType.DMA((5,)),
        ],
        compiler_params=pltpu.CompilerParams(vmem_limit_bytes=60 * 1024 * 1024),
        cost_estimate=pl.CostEstimate(flops=6 * 10**9, bytes_accessed=1, transcendentals=0),
        name="attn_fwd",
    )(where, lengths, place, tokens, *pieces)


def ffn_kernel(e, first, count, whole, tab_ref, tot_ref, where_ref, *rest):
    xs, cs, ws, b_ref = rest[0:8], rest[8:12], rest[12:12 + count], rest[12 + count]
    rest = rest[13 + count:] if first else rest[25 + count:]
    outs, mine_ref, other_ref, gb_ref = rest[:12], rest[12], rest[-15], rest[-14]
    xv, cv, wi, wb, gwi, gwb, xt, ct, ot, dt, in_sems, w_sems, out_sems = rest[-13:]
    y = where_ref[1]
    height = mine_ref.shape[1] // 2
    depth = D // height // 2
    size = cs[0].shape[0]
    weights, tokens = [], []
    for part, target in enumerate((wi, wb)):
        held = pl.ds(part * height, height)
        for n, piece in enumerate(ws):
            place = target if count == 1 else target.at[:, y if n == 0 else 1 - y]
            weights.append(pltpu.make_async_copy(piece.at[:, held], place, w_sems.at[n, part]))
    for n in range(8):
        part = pl.ds(n * (size // 2), size // 2)
        tokens.append(pltpu.make_async_copy(xs[n], xv.at[part], in_sems.at[0, n]))
    for n in range(4):
        tokens.append(pltpu.make_async_copy(cs[n], cv.at[pl.ds(n * size, size)], in_sems.at[1, n]))
    for copy in tokens + weights:
        copy.start()
    gwi[...] = jnp.zeros_like(gwi)
    gwb[...] = jnp.zeros_like(gwb)
    gb_ref[...] = jnp.zeros_like(gb_ref)
    for copy in tokens + weights:
        copy.wait()
    total = tot_ref[0]
    room = size // UNIT

    def pick(low, high, value, found):
        if high - low == 1:
            found(low)
            return
        middle = (low + high) // 2
        lax.cond(
            value < middle, lambda: pick(low, middle, value, found), lambda: pick(middle, high, value, found)
        )

    def send(t, u):
        unit = t * UNITS + u
        held = slice(u * UNIT, (u + 1) * UNIT)

        @pl.when(unit < total)
        def _():
            dst = tab_ref[unit]
            half_of = lax.div(2 * dst, room)

            def found(n):
                for m, (tile_ref, target, first_unit) in enumerate(
                    ((ot, outs[n // 2], n // 2 * room), (dt, outs[4 + n], n * (room // 2)))
                ):
                    rows = pl.ds(pl.multiple_of((dst - first_unit) * UNIT, UNIT), UNIT)
                    pltpu.make_async_copy(tile_ref.at[held], target.at[rows], out_sems.at[m, u]).start()

            pick(0, 8, half_of, found)

    def settle(t, u):
        @pl.when(t * UNITS + u < total)
        def _():
            held = slice(u * UNIT, (u + 1) * UNIT)
            for m, (tile_ref, target) in enumerate(((ot, outs[0]), (dt, outs[4]))):
                pltpu.make_async_copy(tile_ref.at[held], target.at[pl.ds(0, UNIT)], out_sems.at[m, u]).wait()

    def tile(t, carry):
        for u in range(UNITS):
            src = pl.multiple_of(tab_ref[t * UNITS + u] * UNIT, UNIT)
            xt[u * UNIT:(u + 1) * UNIT, :] = xv[pl.ds(src, UNIT), :]
            ct[u * UNIT:(u + 1) * UNIT, :] = cv[pl.ds(src, UNIT), :]
        left = (total - t * UNITS) * UNIT
        row = lax.broadcasted_iota(jnp.int32, (TILE, D), 0)
        part = jnp.where(row < left, ct[...], jnp.zeros_like(ct))
        pre = dot(xt[...], wi[...].reshape(D, -1)) + b_ref[e:e + 1, :]
        share = 0.5 * (1.0 + lax.erf(pre * INV_ROOT_TWO))
        act = (pre * share).astype(BF16)
        slope = share + pre * jnp.exp(-0.5 * pre * pre) * INV_ROOT_TAU

        @pl.when(t > 0)
        def _():
            for u in range(UNITS):
                settle(t - 1, u)

        ot[...] = dot(act, wb[...].reshape(-1, D)).astype(BF16)
        pre_grad = (dot_nt(part, wb[...].reshape(-1, D)) * slope).astype(BF16)
        dt[...] = dot_nt(pre_grad, wi[...].reshape(D, -1)).astype(BF16)
        for u in range(UNITS):
            send(t, u)
        gwb[...] += dot_tn(act, part)
        gwi[...] += dot_tn(xt[...], pre_grad)
        gb_ref[...] += jnp.sum(pre_grad.astype(F32), axis=0, keepdims=True)
        return carry

    tiles = (total + UNITS - 1) // UNITS
    lax.fori_loop(0, tiles, tile, 0)

    @pl.when(tiles > 0)
    def _():
        for u in range(UNITS):
            settle(tiles - 1, u)

    if whole:
        for b in range(2 * depth):
            mine_ref[b, :height, :] = gwi[b * height:(b + 1) * height, :].astype(BF16)
            mine_ref[b, height:, :] = gwb[b * height:(b + 1) * height, :].astype(BF16)
        return
    for z in range(depth):
        for y_of in range(2):
            rows = slice((2 * z + y_of) * height, (2 * z + y_of + 1) * height)
            for flag, target in ((y == y_of, mine_ref), (y != y_of, other_ref)):
                @pl.when(flag)
                def _():
                    target[z, :height, :] = gwi[rows, :].astype(BF16)
                    target[z, height:, :] = gwb[rows, :].astype(BF16)


def ffn(e, table, total, where, xs, cs, weights, bias, before, whole):
    size = cs[0].shape[0]
    first = before is None
    quarter = bias.shape[1]
    tokens = [jax.ShapeDtypeStruct((size, D), BF16)] * 4 + [jax.ShapeDtypeStruct((size // 2, D), BF16)] * 8
    height = weights[0].shape[-2] // 2
    blocked = (D // height, height, D) if len(weights) == 1 else (D // height // 2, 2, height, D)
    blocks = D // height
    grads = [jax.ShapeDtypeStruct((blocks if whole else blocks // 2, 2 * height, D), BF16)] * (1 if whole else 2)
    args = [table, total, where, *xs, *cs, *weights, bias] + ([] if first else list(before))
    return pl.pallas_call(
        functools.partial(ffn_kernel, e, first, len(weights), whole),
        out_shape=(*tokens, *grads, jax.ShapeDtypeStruct((1, quarter), F32)),
        in_specs=[SMEM] * 3 + [ANY] * (12 + len(weights)) + [VMEM] + [ANY] * (0 if first else 12),
        out_specs=(ANY,) * 12 + (VMEM,) * (1 + len(grads)),
        scratch_shapes=[
            pltpu.VMEM((4 * size, D), BF16),
            pltpu.VMEM((4 * size, D), BF16),
            pltpu.VMEM(blocked, BF16),
            pltpu.VMEM(blocked, BF16),
            pltpu.VMEM((D, quarter), F32),
            pltpu.VMEM((quarter, D), F32),
            pltpu.VMEM((TILE, D), BF16),
            pltpu.VMEM((TILE, D), BF16),
            pltpu.VMEM((TILE, D), BF16),
            pltpu.VMEM((TILE, D), BF16),
            pltpu.SemaphoreType.DMA((2, 8)),
            pltpu.SemaphoreType.DMA((len(weights), 2)),
            pltpu.SemaphoreType.DMA((2, UNITS)),
        ],
        input_output_aliases={} if first else {16 + len(weights) + i: i for i in range(12)},
        compiler_params=pltpu.CompilerParams(vmem_limit_bytes=60 * 1024 * 1024),
        cost_estimate=SMALL,
        name="ffn",
    )(*args)


def attn_bwd_kernel(share, where_ref, vec_ref, hot_ref, place_ref, bias_a, bias_b, bias_c, *rest):
    far, outs, held = rest[:11], rest[11:20], rest[20:31]
    gtok_ref, keeps, sends = outs[0], outs[1:5], outs[5:9]
    mg, mxg, dq, dk, dv, gw, gvec_ref, small, sems, out_sems = rest[31:]
    core, y, x = where_ref[0], where_ref[1], where_ref[2]
    leaving = []
    copies = [pltpu.make_async_copy(a, b, sems.at[n]) for n, (a, b) in enumerate(zip(far, held))]
    for copy in copies:
        copy.start()
    dx_a, dx_b, mid, cot, mixed, w_ref, q_ref, k_ref, v_ref, probs_ref, tok = held
    slot = lax.broadcasted_iota(jnp.int32, (tok.shape[0], 2 * dx_a.shape[0]), 1)
    unperm = jnp.where(slot == place_ref[...], 1.0, 0.0).astype(BF16)
    for copy in copies[:4]:
        copy.wait()
    norm2_grad = dot(unperm, jnp.concatenate([dx_a[...], dx_b[...]], axis=0))
    scaled_two, inverse_two = norm_stats(mid[...])
    gvec_ref[3:4, :] = jnp.sum(norm2_grad * scaled_two, axis=0, keepdims=True)
    gvec_ref[4:5, :] = jnp.sum(norm2_grad, axis=0, keepdims=True)
    mid_grad = cot[...].astype(F32) + norm_backward(norm2_grad * vec_ref[3:4, :], scaled_two, inverse_two)
    mg[...] = mid_grad
    branch = mid_grad.astype(BF16)
    gvec_ref[2:3, :] = jnp.sum(branch.astype(F32), axis=0, keepdims=True)
    gvec_ref[5:8, :] = dot(hot_ref[...], cot[...])[:3]
    for copy in copies[4:6]:
        copy.wait()

    def put(matrix, value):
        gw[matrix] = value.astype(BF16).reshape(gw.shape[1:])
        rows = pl.ds((matrix % 2) * (share + 8), share)
        for n in range(4):
            place = 2 * (1 - y if n // 2 else y) + (1 - x if n % 2 else x)
            for flag, target in ((core == matrix // 2, keeps[n]), (core != matrix // 2, sends[n])):
                def copy(target=target, place=place, n=n):
                    return pltpu.make_async_copy(gw.at[matrix, :, place], target.at[:, rows], out_sems.at[matrix, n])

                pl.when(flag)(lambda: copy().start())
                leaving.append((flag, copy))

    put(3, dot_tn(mixed[...], branch))
    mxg[...] = dot_nt(branch, w_ref[3].reshape(D, D)).astype(BF16)
    for copy in copies[6:]:
        copy.wait()
    seqs = tok.shape[0] // SEQ
    scale = HEAD_DIM ** -0.5
    for seq in range(seqs):
        rows = slice(seq * SEQ, (seq + 1) * SEQ)

        def step(pair, carry):
            cols = pl.ds(pl.multiple_of(pair * 128, 128), 128)
            probs = probs_ref[seq * PAIRS + pair]
            grads = two_heads(mxg[rows, cols])
            dv[rows, cols] = dot_tn(probs, grads).astype(BF16)
            prob_grad = dot_nt(grads, v_ref[rows, cols])
            wide = probs.astype(F32)
            inner = jnp.sum(wide * prob_grad, axis=-1, keepdims=True)
            score_grad = (wide * (prob_grad - inner)).astype(BF16)
            dq[rows, cols] = (merge_heads(dot(score_grad, k_ref[rows, cols])) * scale).astype(BF16)
            dk[rows, cols] = (dot_tn(score_grad, two_heads(q_ref[rows, cols])) * scale).astype(BF16)
            return carry

        lax.fori_loop(0, PAIRS, step, 0, unroll=3)
    scaled, inverse = norm_stats(tok[...].astype(F32))
    normed = (scaled * vec_ref[0:1, :] + vec_ref[1:2, :]).astype(BF16)
    put(0, dot_tn(normed, dq[...]))
    put(1, dot_tn(normed, dk[...]))
    put(2, dot_tn(normed, dv[...]))
    norm1_grad = dot_nt(dq[...], w_ref[0].reshape(D, D)) + dot_nt(dk[...], w_ref[1].reshape(D, D)) + dot_nt(dv[...], w_ref[2].reshape(D, D))
    gvec_ref[0:1, :] = jnp.sum(norm1_grad * scaled, axis=0, keepdims=True)
    gvec_ref[1:2, :] = jnp.sum(norm1_grad, axis=0, keepdims=True)
    bias = jnp.concatenate([bias_a[...], bias_b[...], bias_c[...], jnp.zeros((5, D), F32)], axis=0)
    scatter_small(share, core, y, x, gvec_ref[...], bias, small)
    for n in range(4):
        for m, target in enumerate((keeps[n], sends[n])):
            copy = pltpu.make_async_copy(small.at[n], target.at[:, pl.ds(share, 8)], out_sems.at[4 + m, n])
            copy.start()
            leaving.append((None, copy))
    gtok_ref[...] = (mg[...] + norm_backward(norm1_grad * vec_ref[0:1, :], scaled, inverse)).astype(BF16)
    for flag, copy in leaving:
        if flag is None:
            copy.wait()
        else:
            pl.when(flag)(lambda copy=copy: copy().wait())


def attn_bwd(share, where, vec, hot, place, bias_grads, far):
    rows = far[-1].shape[0]
    depth = D // share // 4
    part = jax.ShapeDtypeStruct((depth, 2 * share + 8, D), BF16)
    return pl.pallas_call(
        functools.partial(attn_bwd_kernel, share),
        out_shape=(jax.ShapeDtypeStruct((rows, D), BF16),) + (part,) * 8,
        in_specs=[SMEM] + [VMEM] * 6 + [ANY] * 11,
        out_specs=(VMEM,) + (ANY,) * 8,
        scratch_shapes=[pltpu.VMEM(item.shape, item.dtype) for item in far]
        + [pltpu.VMEM((rows, D), F32)] + [pltpu.VMEM((rows, D), BF16)] * 4
        + [
            pltpu.VMEM((4, depth, 4, share, D), BF16),
            pltpu.VMEM((8, D), F32),
            pltpu.VMEM((4, depth, 8, D), BF16),
            pltpu.SemaphoreType.DMA((11,)),
            pltpu.SemaphoreType.DMA((6, 4)),
        ],
        compiler_params=pltpu.CompilerParams(vmem_limit_bytes=60 * 1024 * 1024),
        cost_estimate=SMALL,
        name="attn_bwd",
    )(where, vec, hot, place, *bias_grads, *far)


def swap(value, axis):
    return lax.ppermute(value, axis, [(0, 1), (1, 0)])


def diagonal(value):
    return lax.ppermute(value, ("y", "x"), [(i, 3 - i) for i in range(4)])


def after_kernel(*refs):
    pass


def after(value, *others):
    return pl.pallas_call(
        after_kernel,
        out_shape=jax.ShapeDtypeStruct(value.shape, value.dtype),
        in_specs=[ANY] * (1 + len(others)),
        out_specs=ANY,
        input_output_aliases={0: 0},
        cost_estimate=SMALL,
        name="after",
    )(value, *others)


def ordered(mine, other, index, axis):
    first = jnp.where(index == 0, mine, other)
    second = jnp.where(index == 0, other, mine)
    return jnp.stack([first, second], axis=axis)


def spread(block, count, *wait):
    copies = jnp.broadcast_to(block[None], (count,) + block.shape)
    return lax.all_to_all(after(copies, *wait) if wait else copies, "z", 0, 0, tiled=True)


def halves(value, index, axis):
    mine = lax.dynamic_index_in_dim(value, index, axis, keepdims=False)
    other = lax.dynamic_index_in_dim(value, 1 - index, axis, keepdims=False)
    return mine, other


def running(values, axis):
    steps = [lax.index_in_dim(values, 0, axis, keepdims=False)]
    for i in range(1, values.shape[axis]):
        steps.append(steps[-1] + lax.index_in_dim(values, i, axis, keepdims=False))
    return jnp.stack(steps, axis=axis)


def add_low(a, b):
    return (a.astype(F32) + b.astype(F32)).astype(BF16)


def body(outer, depth, tokens, modality, lengths, ln1_gain, ln1_bias, w_qkv, w_out, out_bias, ln2_gain, ln2_bias,
         w_in, in_bias, w_back, back_bias, cotangent):
    rows = tokens.shape[0]
    share = w_qkv.shape[0]
    hidden = in_bias.shape[1]
    half = hidden // 2
    planes = 2 * depth
    core = lax.axis_index("c")
    y = lax.axis_index("y")
    x = lax.axis_index("x")

    hot = modality.astype(F32)
    before = jnp.arange(rows, dtype=jnp.int32)
    triangle = (before[None, :] < before[:, None]).astype(BF16)
    rank = dot(triangle, hot.astype(BF16))
    counts = jnp.sum(modality, axis=0)
    units = (counts + UNIT - 1) // UNIT
    starts = running(units, 0) - units
    place = jnp.sum(hot * (rank + (starts * UNIT).astype(F32)[None, :]), axis=1).astype(jnp.int32)
    room = rows // UNIT + EXPERTS - 1
    slots = jnp.arange(room * UNIT, dtype=jnp.int32)
    perm = (slots[:, None] == place[None, :]).astype(BF16)
    unperm = (place[:, None] == slots[None, :]).astype(BF16)
    cs = dot(perm, cotangent).astype(BF16)

    parts = [w_qkv[:, :D], w_qkv[:, D:2 * D], w_qkv[:, 2 * D:], w_out]
    mat_a = jnp.where(core == 0, parts[0], parts[2])
    mat_b = jnp.where(core == 0, parts[1], parts[3])
    small = jnp.stack([ln1_gain, ln1_bias, out_bias, ln2_gain, ln2_bias, back_bias[0], back_bias[1], back_bias[2]])
    small = jnp.pad(small, ((0, 0), (0, SMALL_LANES - share)))
    small = jnp.concatenate([small, jnp.pad(in_bias, ((0, 5), (0, D - SMALL_LANES - hidden)))], axis=1)
    message = jnp.concatenate([mat_a, small, mat_b], axis=0)
    cut = share + 8
    first = after(spread(message, depth), cs)
    near = [first, swap(first, "x"), swap(first, "y"), diagonal(first)]
    pieces = near + [swap(piece, "c") for piece in near]
    def four(value):
        beside = swap(value, "x")
        return [value, beside, swap(value, "c"), swap(beside, "c")]

    units_all = jnp.stack(four(units.astype(F32))).astype(jnp.int32)
    starts_all = running(units_all, 1) - units_all + (jnp.arange(4, dtype=jnp.int32) * room)[:, None]
    ends = running(units_all, 0)
    begins = ends - units_all
    totals = ends[3]
    index = jnp.arange(4 * rows // UNIT + UNITS, dtype=jnp.int32)[:, None, None]
    inside = (index >= begins[None]) & (index < ends[None])
    table = jnp.sum(jnp.where(inside, starts_all[None] + index - begins[None], 0), axis=1).T

    cs_all = four(after(cs, near[3]))

    columns = w_in.reshape(EXPERTS, share, planes, 2, 2, half)
    columns = lax.dynamic_index_in_dim(columns, core, 4, keepdims=False)
    in_mine, in_other = halves(columns, x, 3)
    in_mine = in_mine.reshape(EXPERTS, share, planes * half)
    in_other = in_other.reshape(EXPERTS, share, planes * half)
    in_pair = ordered(in_mine, swap(in_other, "x"), x, 1).reshape(EXPERTS, 2 * share, planes * half)
    back_mine = lax.dynamic_slice_in_dim(w_back, core * half, half, 1)
    block = [jnp.concatenate([in_pair[e], back_mine[e]], axis=0) for e in range(EXPERTS)]
    blocks = (planes, 2 * share + half, D)
    beside = swap(jnp.concatenate([in_mine[2], back_mine[2]], axis=0), "y")
    beside_in = ordered(beside[:share], diagonal(in_other[2]), x, 0).reshape(2 * share, planes * half)
    beside = jnp.concatenate([beside_in, beside[share:]], axis=0)
    first_in = spread(block[0], depth, pieces[4])
    second_in = spread(block[1], depth, *near[1:])
    third = lax.all_gather(after(ordered(block[2], beside, y, 0), *near[1:]), "z", axis=0).reshape(blocks)

    where = jnp.stack([core, y, x]).astype(jnp.int32)
    middle, *xs, q, k, v, mixed, probs, weights, vec, bias_mine = attn_fwd(
        where, lengths, after(place[None, :], first_in), tokens, pieces, share, room
    )
    xs_all = [item for pair in zip(*(four(part) for part in xs)) for item in pair]

    state = None
    grads, bias_grads = [None] * EXPERTS, [None] * EXPERTS
    second_in = after(second_in, xs_all[2])
    first_in = after(first_in, xs[0])
    experts = [[first_in, swap(first_in, "y")], [second_in, swap(second_in, "y")], [third]]
    for e in range(EXPERTS):
        *results, bias_grads[e] = ffn(
            e, table[e], totals[e][None], where, xs_all, cs_all, experts[e], bias_mine, state, e != 2
        )
        state, grads[e] = results[:12], results[12:]
    used = (jnp.sum(units) * UNIT).astype(jnp.int32)

    def pair_sums(own, beside, across, corner):
        beside = add_low(beside, swap(corner, "c"))
        return add_low(own, swap(across, "c")), beside

    def home(own, beside, first=0):
        total = own.astype(F32) + swap(beside, "x").astype(F32)
        line = slots[first:first + own.shape[0], None]
        return jnp.where(line < used, total, 0.0).astype(BF16)

    def scatter_z(parts):
        return lax.all_to_all(parts.reshape(depth, -1, D), "z", 0, 0, tiled=True)

    last = scatter_z(grads[1][0])
    other_sum = swap(grads[2][1], "y")
    shard_low = lax.psum_scatter(grads[0][0], ("z", "y"), scatter_dimension=0)
    dx_pairs = [pair_sums(*state[4 + part::2]) for part in range(2)]
    out_pair = pair_sums(*state[:4])
    dxs = [home(*pair, part * room * UNIT // 2) for part, pair in enumerate(dx_pairs)]
    dxs[0] = after(dxs[0], out_pair[1])

    hot_rows = jnp.pad(jnp.transpose(modality.astype(BF16)), ((0, 5), (0, 0)))
    grad_tokens, *parts = attn_bwd(
        share, where, vec, hot_rows, place[:, None], bias_grads,
        (*dxs, middle, cotangent, mixed, weights, q, k, v, probs, tokens),
    )
    outs = home(*out_pair)
    output = (middle + dot(unperm, outs) + dot(hot.astype(BF16), vec[5:8].astype(BF16))).astype(BF16)

    summed = [add_low(parts[n], swap(parts[4 + n], "c")) for n in (3, 1, 2, 0)]
    summed[0] = after(summed[0], shard_low)
    moved = [diagonal(summed[0]), swap(summed[1], "x"), swap(summed[2], "y"), summed[3]]
    part = (moved[0].astype(F32) + moved[1].astype(F32) + moved[2].astype(F32) + moved[3].astype(F32)).astype(BF16)
    last = jnp.sum(after(last, summed[3]).astype(F32), axis=0).reshape(2, -1, D)
    mine, other = halves(last, y, 0)
    last = mine + swap(other.astype(BF16), "y").astype(F32)
    other_sum = scatter_z(add_low(after(grads[2][0], grad_tokens), other_sum))
    shards = [shard_low.astype(F32), last, jnp.sum(other_sum.astype(F32), axis=0)]
    done = lax.all_to_all(part, "z", 0, 0, tiled=True)
    done = jnp.sum(done.astype(F32), axis=0)
    small = done[share:cut]
    done_low = done.astype(BF16)
    pair = jnp.stack([done_low[:share], done_low[cut:]])
    away = swap(pair, "c")
    grad_q = jnp.where(core == 0, pair[0], away[0])
    grad_k = jnp.where(core == 0, pair[1], away[1])
    grad_v = jnp.where(core == 0, away[0], pair[0])
    grad_o = jnp.where(core == 0, away[1], pair[1])
    grad_w_qkv = jnp.concatenate([grad_q, grad_k, grad_v], axis=1)

    shards = jnp.stack(shards).astype(BF16)
    in_mine, in_other = halves(shards[:, :2 * share].reshape(EXPERTS, 2, share, D), x, 1)
    in_pair = ordered(in_mine, swap(in_other, "x"), x, 2)
    in_pair_c, back_c = swap(in_pair, "c"), swap(shards[:, 2 * share:], "c")
    grad_w_in = ordered(in_pair, in_pair_c, core, 3)
    grad_w_in = grad_w_in.reshape(EXPERTS, share, 2, 2, planes, half)
    grad_w_in = jnp.transpose(grad_w_in, (0, 1, 4, 2, 3, 5)).reshape(EXPERTS, share, 2 * planes * hidden)
    grad_w_back = ordered(shards[:, 2 * share:], back_c, core, 1).reshape(EXPERTS, hidden, D)

    result = (
        small[0, :share], small[1, :share], grad_w_qkv, grad_o, small[2, :share], small[3, :share], small[4, :share],
        grad_w_in, small[:EXPERTS, SMALL_LANES:SMALL_LANES + hidden], grad_w_back, small[5:8, :share],
    )
    if outer > 1:
        result = tuple(lax.psum(item.astype(BF16), "ro") for item in result)
    return (output, grad_tokens) + tuple(item.astype(F32) for item in result)


def solution(mesh):
    reps, shards = mesh.shape["rep"], mesh.shape["fsdp"]
    grid = Mesh(mesh.devices.reshape(reps // 2, 2, shards // 4, 2, 2), ("ro", "c", "z", "y", "x"))
    fsdp = ("z", "y", "x")
    every = ("ro", "c", "z", "y", "x")
    vector, matrix, stack, lines = P(fsdp), P(fsdp, None), P(None, fsdp, None), P(None, fsdp)
    placed = (
        P(every, None), P(every, None), P(every), vector, vector, matrix, matrix, vector, vector, vector,
        stack, lines, stack, lines, P(every, None),
    )
    out = (
        P(every, None), P(every, None), vector, vector, matrix, matrix, vector, vector, vector,
        stack, lines, stack, lines,
    )
    return jax.shard_map(
        functools.partial(body, reps // 2, shards // 4), mesh=grid, in_specs=placed, out_specs=out, check_vma=False
    )
```

```python
import functools
import math

import jax
import jax.numpy as jnp
from jax import lax
from jax.experimental import pallas as pl
from jax.experimental.pallas import tpu as pltpu
from jax.sharding import Mesh
from jax.sharding import PartitionSpec as P

HEADS = 12
HEAD_DIM = 64
SEQ = 256
D = 768
EXPERTS = 3
UNIT = 16
TILE = 256
UNITS = TILE // UNIT

INV_ROOT_TWO = 1.0 / math.sqrt(2.0)
INV_ROOT_TAU = 1.0 / math.sqrt(2.0 * math.pi)
F32 = jnp.float32
BF16 = jnp.bfloat16

VMEM = pl.BlockSpec(memory_space=pltpu.VMEM)
SMEM = pl.BlockSpec(memory_space=pltpu.SMEM)
ANY = pl.BlockSpec(memory_space=pl.ANY)

SMALL_LANES = 128
SMALL = pl.CostEstimate(flops=1, bytes_accessed=1, transcendentals=0)


def dot(a, b):
    return lax.dot_general(a, b, (((1,), (0,)), ((), ())), preferred_element_type=F32)


def dot_nt(a, b):
    return lax.dot_general(a, b, (((1,), (1,)), ((), ())), preferred_element_type=F32)


def dot_tn(a, b):
    return lax.dot_general(a, b, (((0,), (0,)), ((), ())), preferred_element_type=F32)


def norm_stats(values):
    average = jnp.mean(values, axis=-1, keepdims=True)
    centred = values - average
    inverse = lax.rsqrt(jnp.mean(centred * centred, axis=-1, keepdims=True) + 1e-05)
    return centred * inverse, inverse


def norm_backward(weighted, scaled, inverse):
    first = jnp.mean(weighted, axis=-1, keepdims=True)
    second = jnp.mean(weighted * scaled, axis=-1, keepdims=True)
    return inverse * (weighted - first - scaled * second)


def two_heads(block):
    low = lax.broadcasted_iota(jnp.int32, block.shape, 1) < HEAD_DIM
    nothing = jnp.zeros_like(block)
    return jnp.concatenate([jnp.where(low, block, nothing), jnp.where(low, nothing, block)], axis=0)


def merge_heads(block):
    low = lax.broadcasted_iota(jnp.int32, (SEQ, 2 * HEAD_DIM), 1) < HEAD_DIM
    return jnp.where(low, block[:SEQ], block[SEQ:])


PAIRS = HEADS // 2


def attn_fwd_kernel(share, where_ref, len_ref, place_ref, tok_ref, *rest):
    pieces = rest[:8]
    mid_ref, xs_a, xs_b, q_ref, k_ref, v_ref, mixed_ref, probs_ref, w_ref, vec_ref, bias_ref = rest[8:19]
    tok, low, sems, own_sems = rest[19:]
    fetch_tok = pltpu.make_async_copy(tok_ref, tok, own_sems.at[0])
    fetch_tok.start()
    fetch_low = [
        pltpu.make_async_copy(pieces[n].at[:, pl.ds(share, 8)], low.at[n], own_sems.at[1 + n]) for n in range(4)
    ]
    for copy in fetch_low:
        copy.start()
    core, y, x = where_ref[0], where_ref[1], where_ref[2]
    copies = ([], [])
    for matrix in range(2):
        for n, piece in enumerate(pieces):
            far, y_of, x_of = n // 4, (n // 2) % 2, n % 2
            slot = 2 * jnp.where(far == 1, 1 - core, core) + matrix
            place = 2 * jnp.where(y_of == 1, 1 - y, y) + jnp.where(x_of == 1, 1 - x, x)
            copies[matrix].append(pltpu.make_async_copy(
                piece.at[:, pl.ds(matrix * (share + 8), share)], w_ref.at[slot, :, place], sems.at[matrix, n]))
    for copy in copies[0] + copies[1]:
        copy.start()

    def weight(slot):
        return w_ref[slot].reshape(D, D)

    for copy in fetch_low:
        copy.wait()
    gather_small(share, core, y, x, low, vec_ref, bias_ref)
    fetch_tok.wait()
    values = tok[...].astype(F32)
    scaled, _ = norm_stats(values)
    normed = (scaled * vec_ref[0:1, :] + vec_ref[1:2, :]).astype(BF16)
    for copy in copies[0]:
        copy.wait()
    q_ref[...] = dot(normed, weight(0)).astype(BF16)
    v_ref[...] = dot(normed, weight(2)).astype(BF16)
    for copy in copies[1]:
        copy.wait()
    k_ref[...] = dot(normed, weight(1)).astype(BF16)
    seqs = tok_ref.shape[0] // SEQ
    for seq in range(seqs):
        length = len_ref[seq]
        rows = slice(seq * SEQ, (seq + 1) * SEQ)

        def step(pair, carry):
            cols = pl.ds(pl.multiple_of(pair * 128, 128), 128)
            both = two_heads(q_ref[rows, cols])
            scores = dot_nt(both, k_ref[rows, cols]) * (HEAD_DIM ** -0.5)
            valid = lax.broadcasted_iota(jnp.int32, scores.shape, 1) < length
            scores = jnp.where(valid, scores, -1e30)
            top = jnp.max(scores, axis=-1, keepdims=True)
            grown = jnp.exp(scores - top)
            total = jnp.sum(grown, axis=-1, keepdims=True)
            probs = (grown * (1.0 / total)).astype(BF16)
            probs_ref[seq * PAIRS + pair] = probs
            mixed_ref[rows, cols] = merge_heads(dot(probs, v_ref[rows, cols])).astype(BF16)
            return carry

        lax.fori_loop(0, PAIRS, step, 0, unroll=True)
    middle = tok[...].astype(F32) + dot(mixed_ref[...], weight(3)) + vec_ref[2:3, :]
    mid_ref[...] = middle
    scaled_two, _ = norm_stats(middle)
    normed_two = (scaled_two * vec_ref[3:4, :] + vec_ref[4:5, :]).astype(BF16)
    for n, target in enumerate((xs_a, xs_b)):
        slot = lax.broadcasted_iota(jnp.int32, (target.shape[0], tok.shape[0]), 0) + n * target.shape[0]
        perm = jnp.where(slot == place_ref[...], 1.0, 0.0).astype(BF16)
        target[...] = dot(perm, normed_two).astype(BF16)


def gather_small(share, core, y, x, low, vec_ref, bias_ref):
    depth = low.shape[1]
    half = D // (2 * depth)
    lane = lax.broadcasted_iota(jnp.int32, (8, D), 1)
    bias_lane = SMALL_LANES + core * half
    vec = jnp.zeros((8, D), F32)
    bias = jnp.zeros((8, D), F32)
    for n in range(4):
        place_y = 1 - y if n // 2 else y
        place_x = 1 - x if n % 2 else x
        for z in range(depth):
            rows = low[n, z].astype(F32)
            shift = (4 * z + 2 * place_y + place_x) * share
            vec += pltpu.roll(jnp.where(lane < share, rows, 0.0), shift, 1)
            if n % 2 == 0:
                mine = jnp.where((lane >= bias_lane) & (lane < bias_lane + half), rows, 0.0)
                bias += pltpu.roll(mine, lax.rem((2 * z + place_y) * half - bias_lane + D, D), 1)
    vec_ref[...] = vec
    bias_ref[...] = bias


def scatter_small(share, core, y, x, vec, bias, low):
    depth = low.shape[1]
    half = D // (2 * depth)
    lane = lax.broadcasted_iota(jnp.int32, (8, D), 1)
    bias_lane = SMALL_LANES + core * half
    for n in range(4):
        place_y = 1 - y if n // 2 else y
        place_x = 1 - x if n % 2 else x
        for z in range(depth):
            shift = (4 * z + 2 * place_y + place_x) * share
            rows = jnp.where(lane < share, pltpu.roll(vec, lax.rem(D - shift, D), 1), 0.0)
            if n % 2 == 0:
                mine = pltpu.roll(bias, lax.rem(bias_lane - (2 * z + place_y) * half + D, D), 1)
                rows += jnp.where((lane >= bias_lane) & (lane < bias_lane + half), mine, 0.0)
            low[n, z] = rows.astype(BF16)


def attn_fwd(where, lengths, place, tokens, pieces, share, room):
    rows = tokens.shape[0]
    seqs = rows // SEQ
    low = jax.ShapeDtypeStruct((rows, D), BF16)
    return pl.pallas_call(
        functools.partial(attn_fwd_kernel, share),
        out_shape=(
            jax.ShapeDtypeStruct((rows, D), F32),
            jax.ShapeDtypeStruct((room * UNIT // 2, D), BF16),
            jax.ShapeDtypeStruct((room * UNIT // 2, D), BF16),
            low, low, low, low,
            jax.ShapeDtypeStruct((seqs * PAIRS, 2 * SEQ, SEQ), BF16),
            jax.ShapeDtypeStruct((4, pieces[0].shape[0], 4, share, D), BF16),
            jax.ShapeDtypeStruct((8, D), F32),
            jax.ShapeDtypeStruct((8, D), F32),
        ),
        in_specs=[SMEM] * 2 + [VMEM] + [ANY] * 9,
        out_specs=(VMEM,) * 11,
        scratch_shapes=[
            pltpu.VMEM(tokens.shape, BF16),
            pltpu.VMEM((4, pieces[0].shape[0], 8, D), BF16),
            pltpu.SemaphoreType.DMA((2, 8)),
            pltpu.SemaphoreType.DMA((5,)),
        ],
        compiler_params=pltpu.CompilerParams(vmem_limit_bytes=60 * 1024 * 1024),
        cost_estimate=pl.CostEstimate(flops=6 * 10**9, bytes_accessed=1, transcendentals=0),
        name="attn_fwd",
    )(where, lengths, place, tokens, *pieces)


def ffn_kernel(e, first, count, whole, tab_ref, tot_ref, where_ref, *rest):
    xs, cs, ws, b_ref = rest[0:8], rest[8:12], rest[12:12 + count], rest[12 + count]
    rest = rest[13 + count:] if first else rest[25 + count:]
    outs, mine_ref, other_ref, gb_ref = rest[:12], rest[12], rest[-15], rest[-14]
    xv, cv, wi, wb, gwi, gwb, xt, ct, ot, dt, in_sems, w_sems, out_sems = rest[-13:]
    y = where_ref[1]
    height = mine_ref.shape[1] // 2
    depth = D // height // 2
    size = cs[0].shape[0]
    weights, tokens = [], []
    for part, target in enumerate((wi, wb)):
        held = pl.ds(part * height, height)
        for n, piece in enumerate(ws):
            place = target if count == 1 else target.at[:, y if n == 0 else 1 - y]
            weights.append(pltpu.make_async_copy(piece.at[:, held], place, w_sems.at[n, part]))
    for n in range(8):
        part = pl.ds(n * (size // 2), size // 2)
        tokens.append(pltpu.make_async_copy(xs[n], xv.at[part], in_sems.at[0, n]))
    for n in range(4):
        tokens.append(pltpu.make_async_copy(cs[n], cv.at[pl.ds(n * size, size)], in_sems.at[1, n]))
    for copy in tokens + weights:
        copy.start()
    gwi[...] = jnp.zeros_like(gwi)
    gwb[...] = jnp.zeros_like(gwb)
    gb_ref[...] = jnp.zeros_like(gb_ref)
    for copy in tokens + weights:
        copy.wait()
    total = tot_ref[0]
    room = size // UNIT

    def pick(low, high, value, found):
        if high - low == 1:
            found(low)
            return
        middle = (low + high) // 2
        lax.cond(
            value < middle, lambda: pick(low, middle, value, found), lambda: pick(middle, high, value, found)
        )

    def send(t, u):
        unit = t * UNITS + u
        held = slice(u * UNIT, (u + 1) * UNIT)

        @pl.when(unit < total)
        def _():
            dst = tab_ref[unit]
            half_of = lax.div(2 * dst, room)

            def found(n):
                for m, (tile_ref, target, first_unit) in enumerate(
                    ((ot, outs[n // 2], n // 2 * room), (dt, outs[4 + n], n * (room // 2)))
                ):
                    rows = pl.ds(pl.multiple_of((dst - first_unit) * UNIT, UNIT), UNIT)
                    pltpu.make_async_copy(tile_ref.at[held], target.at[rows], out_sems.at[m, u]).start()

            pick(0, 8, half_of, found)

    def settle(t, u):
        @pl.when(t * UNITS + u < total)
        def _():
            held = slice(u * UNIT, (u + 1) * UNIT)
            for m, (tile_ref, target) in enumerate(((ot, outs[0]), (dt, outs[4]))):
                pltpu.make_async_copy(tile_ref.at[held], target.at[pl.ds(0, UNIT)], out_sems.at[m, u]).wait()

    def tile(t, carry):
        for u in range(UNITS):
            src = pl.multiple_of(tab_ref[t * UNITS + u] * UNIT, UNIT)
            xt[u * UNIT:(u + 1) * UNIT, :] = xv[pl.ds(src, UNIT), :]
            ct[u * UNIT:(u + 1) * UNIT, :] = cv[pl.ds(src, UNIT), :]
        left = (total - t * UNITS) * UNIT
        row = lax.broadcasted_iota(jnp.int32, (TILE, D), 0)
        part = jnp.where(row < left, ct[...], jnp.zeros_like(ct))
        pre = dot(xt[...], wi[...].reshape(D, -1)) + b_ref[e:e + 1, :]
        share = 0.5 * (1.0 + lax.erf(pre * INV_ROOT_TWO))
        act = (pre * share).astype(BF16)
        slope = share + pre * jnp.exp(-0.5 * pre * pre) * INV_ROOT_TAU

        @pl.when(t > 0)
        def _():
            for u in range(UNITS):
                settle(t - 1, u)

        ot[...] = dot(act, wb[...].reshape(-1, D)).astype(BF16)
        pre_grad = (dot_nt(part, wb[...].reshape(-1, D)) * slope).astype(BF16)
        dt[...] = dot_nt(pre_grad, wi[...].reshape(D, -1)).astype(BF16)
        for u in range(UNITS):
            send(t, u)
        gwb[...] += dot_tn(act, part)
        gwi[...] += dot_tn(xt[...], pre_grad)
        gb_ref[...] += jnp.sum(pre_grad.astype(F32), axis=0, keepdims=True)
        return carry

    tiles = (total + UNITS - 1) // UNITS
    lax.fori_loop(0, tiles, tile, 0)

    @pl.when(tiles > 0)
    def _():
        for u in range(UNITS):
            settle(tiles - 1, u)

    if whole:
        for b in range(2 * depth):
            mine_ref[b, :height, :] = gwi[b * height:(b + 1) * height, :].astype(BF16)
            mine_ref[b, height:, :] = gwb[b * height:(b + 1) * height, :].astype(BF16)
        return
    for z in range(depth):
        for y_of in range(2):
            rows = slice((2 * z + y_of) * height, (2 * z + y_of + 1) * height)
            for flag, target in ((y == y_of, mine_ref), (y != y_of, other_ref)):
                @pl.when(flag)
                def _():
                    target[z, :height, :] = gwi[rows, :].astype(BF16)
                    target[z, height:, :] = gwb[rows, :].astype(BF16)


def ffn(e, table, total, where, xs, cs, weights, bias, before, whole):
    size = cs[0].shape[0]
    first = before is None
    quarter = bias.shape[1]
    tokens = [jax.ShapeDtypeStruct((size, D), BF16)] * 4 + [jax.ShapeDtypeStruct((size // 2, D), BF16)] * 8
    height = weights[0].shape[-2] // 2
    blocked = (D // height, height, D) if len(weights) == 1 else (D // height // 2, 2, height, D)
    blocks = D // height
    grads = [jax.ShapeDtypeStruct((blocks if whole else blocks // 2, 2 * height, D), BF16)] * (1 if whole else 2)
    args = [table, total, where, *xs, *cs, *weights, bias] + ([] if first else list(before))
    return pl.pallas_call(
        functools.partial(ffn_kernel, e, first, len(weights), whole),
        out_shape=(*tokens, *grads, jax.ShapeDtypeStruct((1, quarter), F32)),
        in_specs=[SMEM] * 3 + [ANY] * (12 + len(weights)) + [VMEM] + [ANY] * (0 if first else 12),
        out_specs=(ANY,) * 12 + (VMEM,) * (1 + len(grads)),
        scratch_shapes=[
            pltpu.VMEM((4 * size, D), BF16),
            pltpu.VMEM((4 * size, D), BF16),
            pltpu.VMEM(blocked, BF16),
            pltpu.VMEM(blocked, BF16),
            pltpu.VMEM((D, quarter), F32),
            pltpu.VMEM((quarter, D), F32),
            pltpu.VMEM((TILE, D), BF16),
            pltpu.VMEM((TILE, D), BF16),
            pltpu.VMEM((TILE, D), BF16),
            pltpu.VMEM((TILE, D), BF16),
            pltpu.SemaphoreType.DMA((2, 8)),
            pltpu.SemaphoreType.DMA((len(weights), 2)),
            pltpu.SemaphoreType.DMA((2, UNITS)),
        ],
        input_output_aliases={} if first else {16 + len(weights) + i: i for i in range(12)},
        compiler_params=pltpu.CompilerParams(vmem_limit_bytes=60 * 1024 * 1024),
        cost_estimate=SMALL,
        name="ffn",
    )(*args)


def attn_bwd_kernel(share, where_ref, vec_ref, hot_ref, place_ref, bias_a, bias_b, bias_c, *rest):
    far, outs, held = rest[:11], rest[11:20], rest[20:31]
    gtok_ref, keeps, sends = outs[0], outs[1:5], outs[5:9]
    mg, mxg, dq, dk, dv, gw, gvec_ref, small, sems, out_sems = rest[31:]
    core, y, x = where_ref[0], where_ref[1], where_ref[2]
    leaving = []
    copies = [pltpu.make_async_copy(a, b, sems.at[n]) for n, (a, b) in enumerate(zip(far, held))]
    for copy in copies:
        copy.start()
    dx_a, dx_b, mid, cot, mixed, w_ref, q_ref, k_ref, v_ref, probs_ref, tok = held
    slot = lax.broadcasted_iota(jnp.int32, (tok.shape[0], 2 * dx_a.shape[0]), 1)
    unperm = jnp.where(slot == place_ref[...], 1.0, 0.0).astype(BF16)
    for copy in copies[:4]:
        copy.wait()
    norm2_grad = dot(unperm, jnp.concatenate([dx_a[...], dx_b[...]], axis=0))
    scaled_two, inverse_two = norm_stats(mid[...])
    gvec_ref[3:4, :] = jnp.sum(norm2_grad * scaled_two, axis=0, keepdims=True)
    gvec_ref[4:5, :] = jnp.sum(norm2_grad, axis=0, keepdims=True)
    mid_grad = cot[...].astype(F32) + norm_backward(norm2_grad * vec_ref[3:4, :], scaled_two, inverse_two)
    mg[...] = mid_grad
    branch = mid_grad.astype(BF16)
    gvec_ref[2:3, :] = jnp.sum(branch.astype(F32), axis=0, keepdims=True)
    gvec_ref[5:8, :] = dot(hot_ref[...], cot[...])[:3]
    for copy in copies[4:6]:
        copy.wait()

    def put(matrix, value):
        gw[matrix] = value.astype(BF16).reshape(gw.shape[1:])
        rows = pl.ds((matrix % 2) * (share + 8), share)
        for n in range(4):
            place = 2 * (1 - y if n // 2 else y) + (1 - x if n % 2 else x)
            for flag, target in ((core == matrix // 2, keeps[n]), (core != matrix // 2, sends[n])):
                def copy(target=target, place=place, n=n):
                    return pltpu.make_async_copy(gw.at[matrix, :, place], target.at[:, rows], out_sems.at[matrix, n])

                pl.when(flag)(lambda: copy().start())
                leaving.append((flag, copy))

    put(3, dot_tn(mixed[...], branch))
    mxg[...] = dot_nt(branch, w_ref[3].reshape(D, D)).astype(BF16)
    for copy in copies[6:]:
        copy.wait()
    seqs = tok.shape[0] // SEQ
    scale = HEAD_DIM ** -0.5
    for seq in range(seqs):
        rows = slice(seq * SEQ, (seq + 1) * SEQ)

        def step(pair, carry):
            cols = pl.ds(pl.multiple_of(pair * 128, 128), 128)
            probs = probs_ref[seq * PAIRS + pair]
            grads = two_heads(mxg[rows, cols])
            dv[rows, cols] = dot_tn(probs, grads).astype(BF16)
            prob_grad = dot_nt(grads, v_ref[rows, cols])
            wide = probs.astype(F32)
            inner = jnp.sum(wide * prob_grad, axis=-1, keepdims=True)
            score_grad = (wide * (prob_grad - inner)).astype(BF16)
            dq[rows, cols] = (merge_heads(dot(score_grad, k_ref[rows, cols])) * scale).astype(BF16)
            dk[rows, cols] = (dot_tn(score_grad, two_heads(q_ref[rows, cols])) * scale).astype(BF16)
            return carry

        lax.fori_loop(0, PAIRS, step, 0, unroll=True)
    scaled, inverse = norm_stats(tok[...].astype(F32))
    normed = (scaled * vec_ref[0:1, :] + vec_ref[1:2, :]).astype(BF16)
    put(0, dot_tn(normed, dq[...]))
    put(1, dot_tn(normed, dk[...]))
    put(2, dot_tn(normed, dv[...]))
    norm1_grad = dot_nt(dq[...], w_ref[0].reshape(D, D)) + dot_nt(dk[...], w_ref[1].reshape(D, D)) + dot_nt(dv[...], w_ref[2].reshape(D, D))
    gvec_ref[0:1, :] = jnp.sum(norm1_grad * scaled, axis=0, keepdims=True)
    gvec_ref[1:2, :] = jnp.sum(norm1_grad, axis=0, keepdims=True)
    bias = jnp.concatenate([bias_a[...], bias_b[...], bias_c[...], jnp.zeros((5, D), F32)], axis=0)
    scatter_small(share, core, y, x, gvec_ref[...], bias, small)
    for n in range(4):
        for m, target in enumerate((keeps[n], sends[n])):
            copy = pltpu.make_async_copy(small.at[n], target.at[:, pl.ds(share, 8)], out_sems.at[4 + m, n])
            copy.start()
            leaving.append((None, copy))
    gtok_ref[...] = (mg[...] + norm_backward(norm1_grad * vec_ref[0:1, :], scaled, inverse)).astype(BF16)
    for flag, copy in leaving:
        if flag is None:
            copy.wait()
        else:
            pl.when(flag)(lambda copy=copy: copy().wait())


def attn_bwd(share, where, vec, hot, place, bias_grads, far):
    rows = far[-1].shape[0]
    depth = D // share // 4
    part = jax.ShapeDtypeStruct((depth, 2 * share + 8, D), BF16)
    return pl.pallas_call(
        functools.partial(attn_bwd_kernel, share),
        out_shape=(jax.ShapeDtypeStruct((rows, D), BF16),) + (part,) * 8,
        in_specs=[SMEM] + [VMEM] * 6 + [ANY] * 11,
        out_specs=(VMEM,) + (ANY,) * 8,
        scratch_shapes=[pltpu.VMEM(item.shape, item.dtype) for item in far]
        + [pltpu.VMEM((rows, D), F32)] + [pltpu.VMEM((rows, D), BF16)] * 4
        + [
            pltpu.VMEM((4, depth, 4, share, D), BF16),
            pltpu.VMEM((8, D), F32),
            pltpu.VMEM((4, depth, 8, D), BF16),
            pltpu.SemaphoreType.DMA((11,)),
            pltpu.SemaphoreType.DMA((6, 4)),
        ],
        compiler_params=pltpu.CompilerParams(vmem_limit_bytes=60 * 1024 * 1024),
        cost_estimate=SMALL,
        name="attn_bwd",
    )(where, vec, hot, place, *bias_grads, *far)


def swap(value, axis):
    return lax.ppermute(value, axis, [(0, 1), (1, 0)])


def diagonal(value):
    return lax.ppermute(value, ("y", "x"), [(i, 3 - i) for i in range(4)])


def after_kernel(*refs):
    pass


def after(value, *others):
    return pl.pallas_call(
        after_kernel,
        out_shape=jax.ShapeDtypeStruct(value.shape, value.dtype),
        in_specs=[ANY] * (1 + len(others)),
        out_specs=ANY,
        input_output_aliases={0: 0},
        cost_estimate=SMALL,
        name="after",
    )(value, *others)


def ordered(mine, other, index, axis):
    first = jnp.where(index == 0, mine, other)
    second = jnp.where(index == 0, other, mine)
    return jnp.stack([first, second], axis=axis)


def spread(block, count, *wait):
    copies = jnp.broadcast_to(block[None], (count,) + block.shape)
    return lax.all_to_all(after(copies, *wait) if wait else copies, "z", 0, 0, tiled=True)


def halves(value, index, axis):
    mine = lax.dynamic_index_in_dim(value, index, axis, keepdims=False)
    other = lax.dynamic_index_in_dim(value, 1 - index, axis, keepdims=False)
    return mine, other


def running(values, axis):
    steps = [lax.index_in_dim(values, 0, axis, keepdims=False)]
    for i in range(1, values.shape[axis]):
        steps.append(steps[-1] + lax.index_in_dim(values, i, axis, keepdims=False))
    return jnp.stack(steps, axis=axis)


def add_low(a, b):
    return (a.astype(F32) + b.astype(F32)).astype(BF16)


def body(outer, depth, tokens, modality, lengths, ln1_gain, ln1_bias, w_qkv, w_out, out_bias, ln2_gain, ln2_bias,
         w_in, in_bias, w_back, back_bias, cotangent):
    rows = tokens.shape[0]
    share = w_qkv.shape[0]
    hidden = in_bias.shape[1]
    half = hidden // 2
    planes = 2 * depth
    core = lax.axis_index("c")
    y = lax.axis_index("y")
    x = lax.axis_index("x")

    hot = modality.astype(F32)
    before = jnp.arange(rows, dtype=jnp.int32)
    triangle = (before[None, :] < before[:, None]).astype(BF16)
    rank = dot(triangle, hot.astype(BF16))
    counts = jnp.sum(modality, axis=0)
    units = (counts + UNIT - 1) // UNIT
    starts = running(units, 0) - units
    place = jnp.sum(hot * (rank + (starts * UNIT).astype(F32)[None, :]), axis=1).astype(jnp.int32)
    room = rows // UNIT + EXPERTS - 1
    slots = jnp.arange(room * UNIT, dtype=jnp.int32)
    perm = (slots[:, None] == place[None, :]).astype(BF16)
    unperm = (place[:, None] == slots[None, :]).astype(BF16)
    cs = dot(perm, cotangent).astype(BF16)

    parts = [w_qkv[:, :D], w_qkv[:, D:2 * D], w_qkv[:, 2 * D:], w_out]
    mat_a = jnp.where(core == 0, parts[0], parts[2])
    mat_b = jnp.where(core == 0, parts[1], parts[3])
    small = jnp.stack([ln1_gain, ln1_bias, out_bias, ln2_gain, ln2_bias, back_bias[0], back_bias[1], back_bias[2]])
    small = jnp.pad(small, ((0, 0), (0, SMALL_LANES - share)))
    small = jnp.concatenate([small, jnp.pad(in_bias, ((0, 5), (0, D - SMALL_LANES - hidden)))], axis=1)
    message = jnp.concatenate([mat_a, small, mat_b], axis=0)
    cut = share + 8
    first = after(spread(message, depth), cs)
    near = [first, swap(first, "x"), swap(first, "y"), diagonal(first)]
    pieces = near + [swap(piece, "c") for piece in near]
    def four(value):
        beside = swap(value, "x")
        return [value, beside, swap(value, "c"), swap(beside, "c")]

    units_all = jnp.stack(four(units.astype(F32))).astype(jnp.int32)
    starts_all = running(units_all, 1) - units_all + (jnp.arange(4, dtype=jnp.int32) * room)[:, None]
    ends = running(units_all, 0)
    begins = ends - units_all
    totals = ends[3]
    index = jnp.arange(4 * rows // UNIT + UNITS, dtype=jnp.int32)[:, None, None]
    inside = (index >= begins[None]) & (index < ends[None])
    table = jnp.sum(jnp.where(inside, starts_all[None] + index - begins[None], 0), axis=1).T

    cs_all = four(after(cs, near[3]))

    columns = w_in.reshape(EXPERTS, share, planes, 2, 2, half)
    columns = lax.dynamic_index_in_dim(columns, core, 4, keepdims=False)
    in_mine, in_other = halves(columns, x, 3)
    in_mine = in_mine.reshape(EXPERTS, share, planes * half)
    in_other = in_other.reshape(EXPERTS, share, planes * half)
    in_pair = ordered(in_mine, swap(in_other, "x"), x, 1).reshape(EXPERTS, 2 * share, planes * half)
    back_mine = lax.dynamic_slice_in_dim(w_back, core * half, half, 1)
    block = [jnp.concatenate([in_pair[e], back_mine[e]], axis=0) for e in range(EXPERTS)]
    blocks = (planes, 2 * share + half, D)
    beside = swap(jnp.concatenate([in_mine[2], back_mine[2]], axis=0), "y")
    beside_in = ordered(beside[:share], diagonal(in_other[2]), x, 0).reshape(2 * share, planes * half)
    beside = jnp.concatenate([beside_in, beside[share:]], axis=0)
    first_in = spread(block[0], depth, pieces[4])
    second_in = spread(block[1], depth, *near[1:])
    third = lax.all_gather(after(ordered(block[2], beside, y, 0), *near[1:]), "z", axis=0).reshape(blocks)

    where = jnp.stack([core, y, x]).astype(jnp.int32)
    middle, *xs, q, k, v, mixed, probs, weights, vec, bias_mine = attn_fwd(
        where, lengths, after(place[None, :], first_in), tokens, pieces, share, room
    )
    xs_all = [item for pair in zip(*(four(part) for part in xs)) for item in pair]

    state = None
    grads, bias_grads = [None] * EXPERTS, [None] * EXPERTS
    second_in = after(second_in, xs_all[2])
    first_in = after(first_in, xs[0])
    experts = [[first_in, swap(first_in, "y")], [second_in, swap(second_in, "y")], [third]]
    for e in range(EXPERTS):
        *results, bias_grads[e] = ffn(
            e, table[e], totals[e][None], where, xs_all, cs_all, experts[e], bias_mine, state, e != 2
        )
        state, grads[e] = results[:12], results[12:]
    used = (jnp.sum(units) * UNIT).astype(jnp.int32)

    def pair_sums(own, beside, across, corner):
        beside = add_low(beside, swap(corner, "c"))
        return add_low(own, swap(across, "c")), beside

    def home(own, beside, first=0):
        total = own.astype(F32) + swap(beside, "x").astype(F32)
        line = slots[first:first + own.shape[0], None]
        return jnp.where(line < used, total, 0.0).astype(BF16)

    def scatter_z(parts):
        return lax.all_to_all(parts.reshape(depth, -1, D), "z", 0, 0, tiled=True)

    last = scatter_z(grads[1][0])
    other_sum = swap(grads[2][1], "y")
    shard_low = lax.psum_scatter(grads[0][0], ("z", "y"), scatter_dimension=0)
    dx_pairs = [pair_sums(*state[4 + part::2]) for part in range(2)]
    out_pair = pair_sums(*state[:4])
    dxs = [home(*pair, part * room * UNIT // 2) for part, pair in enumerate(dx_pairs)]
    dxs[0] = after(dxs[0], out_pair[1])

    hot_rows = jnp.pad(jnp.transpose(modality.astype(BF16)), ((0, 5), (0, 0)))
    grad_tokens, *parts = attn_bwd(
        share, where, vec, hot_rows, place[:, None], bias_grads,
        (*dxs, middle, cotangent, mixed, weights, q, k, v, probs, tokens),
    )
    outs = home(*out_pair)
    output = (middle + dot(unperm, outs) + dot(hot.astype(BF16), vec[5:8].astype(BF16))).astype(BF16)

    summed = [add_low(parts[n], swap(parts[4 + n], "c")) for n in (3, 1, 2, 0)]
    summed[0] = after(summed[0], shard_low)
    moved = [diagonal(summed[0]), swap(summed[1], "x"), swap(summed[2], "y"), summed[3]]
    part = (moved[0].astype(F32) + moved[1].astype(F32) + moved[2].astype(F32) + moved[3].astype(F32)).astype(BF16)
    last = jnp.sum(after(last, summed[3]).astype(F32), axis=0).reshape(2, -1, D)
    mine, other = halves(last, y, 0)
    last = mine + swap(other.astype(BF16), "y").astype(F32)
    other_sum = scatter_z(add_low(after(grads[2][0], grad_tokens), other_sum))
    shards = [shard_low.astype(F32), last, jnp.sum(other_sum.astype(F32), axis=0)]
    done = lax.all_to_all(part, "z", 0, 0, tiled=True)
    done = jnp.sum(done.astype(F32), axis=0)
    small = done[share:cut]
    done_low = done.astype(BF16)
    pair = jnp.stack([done_low[:share], done_low[cut:]])
    away = swap(pair, "c")
    grad_q = jnp.where(core == 0, pair[0], away[0])
    grad_k = jnp.where(core == 0, pair[1], away[1])
    grad_v = jnp.where(core == 0, away[0], pair[0])
    grad_o = jnp.where(core == 0, away[1], pair[1])
    grad_w_qkv = jnp.concatenate([grad_q, grad_k, grad_v], axis=1)

    shards = jnp.stack(shards).astype(BF16)
    in_mine, in_other = halves(shards[:, :2 * share].reshape(EXPERTS, 2, share, D), x, 1)
    in_pair = ordered(in_mine, swap(in_other, "x"), x, 2)
    in_pair_c, back_c = swap(in_pair, "c"), swap(shards[:, 2 * share:], "c")
    grad_w_in = ordered(in_pair, in_pair_c, core, 3)
    grad_w_in = grad_w_in.reshape(EXPERTS, share, 2, 2, planes, half)
    grad_w_in = jnp.transpose(grad_w_in, (0, 1, 4, 2, 3, 5)).reshape(EXPERTS, share, 2 * planes * hidden)
    grad_w_back = ordered(shards[:, 2 * share:], back_c, core, 1).reshape(EXPERTS, hidden, D)

    result = (
        small[0, :share], small[1, :share], grad_w_qkv, grad_o, small[2, :share], small[3, :share], small[4, :share],
        grad_w_in, small[:EXPERTS, SMALL_LANES:SMALL_LANES + hidden], grad_w_back, small[5:8, :share],
    )
    if outer > 1:
        result = tuple(lax.psum(item.astype(BF16), "ro") for item in result)
    return (output, grad_tokens) + tuple(item.astype(F32) for item in result)


def solution(mesh):
    reps, shards = mesh.shape["rep"], mesh.shape["fsdp"]
    grid = Mesh(mesh.devices.reshape(reps // 2, 2, shards // 4, 2, 2), ("ro", "c", "z", "y", "x"))
    fsdp = ("z", "y", "x")
    every = ("ro", "c", "z", "y", "x")
    vector, matrix, stack, lines = P(fsdp), P(fsdp, None), P(None, fsdp, None), P(None, fsdp)
    placed = (
        P(every, None), P(every, None), P(every), vector, vector, matrix, matrix, vector, vector, vector,
        stack, lines, stack, lines, P(every, None),
    )
    out = (
        P(every, None), P(every, None), vector, vector, matrix, matrix, vector, vector, vector,
        stack, lines, stack, lines,
    )
    return jax.shard_map(
        functools.partial(body, reps // 2, shards // 4), mesh=grid, in_specs=placed, out_specs=out, check_vma=False
    )
```
